1024 devices in a mesh: ctx: 64 (over z, x), dp: 4 (over y_lo), section: 4 (over y_hi, core).
Axes of the slice: x: 8, y: 8 (y_hi: 2, y_lo: 4; y = y_hi * 4 + y_lo), z: 8, core: 2. Of those that a mesh axis runs over, the one named last changes fastest.
Arguments:
- tokens: bfloat16 [4, 4, 8192, 4096], P('section', 'dp', 'ctx'), may hold values from -6 to 6
- norm_gain: float32 [4, 4096], P('section'), may hold values from 0.1 to 1.9
- query_weight: bfloat16 [4, 4096, 512], P('section', 'dp'), may hold values from -0.421875 to 0.421875
- key_weight: bfloat16 [4, 4096, 128], P('section', 'dp'), may hold values from -0.421875 to 0.421875
- value_weight: bfloat16 [4, 4096, 128], P('section', 'dp'), may hold values from -0.09375 to 0.09375
- block_order: int32 [4, 4, 128], P('section', 'dp'), may hold values from 0 to 127, each once within a row
- doc_ids: int32 [4, 4, 8192], P('section', 'dp'), may hold values from 0 to 3, never falling along the last dimension, each value on 1 to 4096 neighbouring positions
Outputs:
- passed: bfloat16 [4, 4, 8192, 512], P('section', 'dp', 'ctx')
The draws below stay inside these ranges and needn't reach their ends.
Inputs may be any that keep to these rules, and one draw needn't show every extreme that they name: `block_order`: each row is a permutation of the block numbers. `doc_ids`: never falling along positions; every document holds 1 to 4096 positions, and one holds exactly 4096.
All inputs are finite; a program needn't handle non-finite values.
Results may differ from the reference program's by a relative error of at most 0.012.
Values may be sent and summed in bfloat16 or wider, within the bound.
A program may use at most 32 MiB of HBM per device.

```python
import math
import jax
import jax.numpy as jnp
import numpy as np
from jax import lax

D = 4096
HEAD = 128
QH = 4
DOCS = 4
HALF = 64
L = 8192
BLOCKS = 128
SECTIONS = 4
SEQS = 4


def draw_query_weight(key, part):
    other = jnp.clip(jax.random.normal(jax.random.fold_in(key, 11), (SECTIONS, D, QH * HEAD), jnp.float32), -6.0, 6.0) / math.sqrt(D)
    return other.astype(jnp.bfloat16)


def draw_key_weight(key, part):
    result = jnp.clip(jax.random.normal(jax.random.fold_in(key, 13), (SECTIONS, D, HEAD), jnp.float32), -6.0, 6.0) / math.sqrt(D)
    return result.astype(jnp.bfloat16)


def draw_tokens(key, part):
    base = jnp.clip(jax.random.normal(jax.random.fold_in(key, 17), (SECTIONS, SEQS, L, D), jnp.float32), -6.0, 6.0)
    return base.astype(jnp.bfloat16)


def block_scale(key, extent, cuts, least, top_value):
    loudness = 1.0
    for position, shards_of in cuts:
        draws = jax.random.uniform(jax.random.fold_in(jax.random.fold_in(key, 6), position), (shards_of,), jnp.float32, least / len(cuts), top_value / len(cuts))
        loudness = loudness * jnp.repeat(jnp.exp(draws), extent[position] // shards_of).reshape((-1,) + (1,) * (len(extent) - 1 - position))
    return loudness


def length_profile(count, total, limit, skew):
    weights = [(1 << 20) // math.isqrt(rank ** skew) + 1 for rank in range(2, count + 1)]
    rest, holding = total - limit - (count - 1), [1] * (count - 1)
    while rest > 0:
        movable = [i for i in range(count - 1) if holding[i] < limit]
        whole, remaining = sum([weights[i] for i in movable]), rest
        for i in movable:
            addition = min(limit - holding[i], max(1, remaining * weights[i] // whole), rest)
            holding[i] = holding[i] + addition
            rest = rest - addition
    return np.array([limit] + holding)


def ragged_sizes(key, count, total, bound, lean):
    if count == 2:
        one = jax.random.randint(key, (), max(1, total - bound), min(bound, total - 1) + 1)
        return jnp.stack([one, total - one])
    tallies = jnp.asarray(length_profile(count, total, bound, lean), jnp.int32)
    pairs = (count - 1) // 2
    source_of, taker = tallies[1:1 + 2 * pairs:2], tallies[2:2 + 2 * pairs:2]
    room = jnp.minimum(source_of - 1, bound - taker)
    passed = jax.random.randint(jax.random.fold_in(key, 1), (pairs,), 0, 1 << 20) % (room + 1)
    tallies = tallies.at[1:1 + 2 * pairs:2].set(source_of - passed).at[2:2 + 2 * pairs:2].set(taker + passed)
    return tallies[jax.random.permutation(jax.random.fold_in(key, 2), count)]


def noise(key, extent, scale, limit, cuts=(), held_as=jnp.bfloat16):
    entries = scale * jax.random.normal(key, extent, jnp.float32)
    if cuts:
        entries = entries * block_scale(key, extent, cuts, -0.22, 0.18)
    return jnp.clip(entries, -limit, limit).astype(held_as)


def setup_inputs(seed: int = 0) -> dict:
    splits = jax.random.split(jax.random.key(seed), 8)
    tokens = draw_tokens(jax.random.fold_in(splits[7], 71), 0)
    norm_gain = jnp.clip(1.0 + 0.18 * jax.random.normal(splits[1], (SECTIONS, D), jnp.float32), 0.1, 1.9)
    query_weight = draw_query_weight(jax.random.fold_in(splits[7], 71), 0)
    key_weight = draw_key_weight(jax.random.fold_in(splits[7], 71), 0)
    value_weight = noise(splits[4], (SECTIONS, D, HEAD), D ** -0.5, 0.09375, ((0, 4), (1, 4)))
    block_order = jax.vmap(lambda own: jax.random.permutation(own, BLOCKS))(jax.random.split(splits[5], SECTIONS * SEQS)).reshape((SECTIONS, SEQS, BLOCKS)).astype(jnp.int32)
    doc_ids = jax.vmap(lambda own: jnp.searchsorted(jnp.cumsum(ragged_sizes(own, DOCS, L, L // 2, 2)), jnp.arange(L), side="right"))(jax.random.split(splits[6], SECTIONS * SEQS)).reshape((SECTIONS, SEQS, L)).astype(jnp.int32)
    return {"tokens": tokens, "norm_gain": norm_gain, "query_weight": query_weight, "key_weight": key_weight, "value_weight": value_weight, "block_order": block_order, "doc_ids": doc_ids}


ROPE_BASE = 500000.0
EPSILON = 1e-05
MASKED = -1e+30

def round_trip(values):
    return lax.optimization_barrier(values.astype(jnp.bfloat16)).astype(jnp.float32)

def rotate_pairs(values, positions, head_size):
    count_rows = values.shape[0]
    shaped = values.reshape(count_rows, -1, head_size)
    halfway = head_size // 2
    freqs = ROPE_BASE ** (-jnp.arange(halfway, dtype=jnp.float32) * 2.0 / head_size)
    angles = positions.astype(jnp.float32)[:, None, None] * freqs[None, None, :]
    cosine = jnp.cos(angles)
    sine = jnp.sin(angles)
    first_half = shaped[..., :halfway]
    second_half = shaped[..., halfway:]
    turned = jnp.concatenate([first_half * cosine - second_half * sine, second_half * cosine + first_half * sine], axis=-1)
    return turned.reshape(count_rows, -1)

def one_sequence(rows, gain_row, query_section, key_section, value_section, order, documents):
    widened = rows.astype(jnp.float32)
    normed = (widened * lax.rsqrt(lax.optimization_barrier(jnp.mean(widened * widened, axis=-1, keepdims=True)) + EPSILON) * gain_row[None, :]).astype(jnp.bfloat16)
    q_raw = jnp.dot(normed, query_section, preferred_element_type=jnp.float32)
    k_raw = jnp.dot(normed, key_section, preferred_element_type=jnp.float32)
    v_raw = jnp.dot(normed, value_section, preferred_element_type=jnp.float32)
    positions = (order[:, None].astype(jnp.int32) * HALF + jnp.arange(HALF, dtype=jnp.int32)[None, :]).reshape(-1)
    row_docs = documents[positions]
    queries = round_trip(rotate_pairs(q_raw, positions, HEAD)).reshape(L, QH, HEAD)
    keys = round_trip(rotate_pairs(k_raw, positions, HEAD))
    values = round_trip(v_raw)
    block = math.gcd(L, 512)

    def one_block(index):
        begin = (index * block).astype(jnp.int32)
        query_block = lax.dynamic_slice_in_dim(queries, begin, block, 0)
        query_pos = lax.dynamic_slice_in_dim(positions, begin, block, 0)
        query_doc = lax.dynamic_slice_in_dim(row_docs, begin, block, 0)
        scores = jnp.einsum('qhd,kd->hqk', query_block, keys) * HEAD ** (-0.5)
        allowed = (row_docs[None, :] == query_doc[:, None]) & (positions[None, :] <= query_pos[:, None])
        scores = jnp.where(allowed[None], scores, MASKED)
        row_max = lax.optimization_barrier(jnp.max(scores, axis=-1))
        probs = jnp.where(allowed[None], jnp.exp(scores - row_max[..., None]), 0.0)
        total = lax.optimization_barrier(jnp.sum(probs, axis=-1))
        numer = jnp.einsum('hqk,kd->hqd', round_trip(probs), values)
        result = numer / total[..., None]
        return result.transpose(1, 0, 2).reshape(block, QH * HEAD).astype(jnp.bfloat16)
    blocks = lax.map(one_block, jnp.arange(L // block, dtype=jnp.int32))
    return blocks.reshape(L, QH * HEAD)

def reference(tokens, norm_gain, query_weight, key_weight, value_weight, block_order, doc_ids):
    section_outputs = []
    for section in range(SECTIONS):
        sequence_outputs = []
        for sequence in range(SEQS):
            sequence_outputs.append(one_sequence(tokens[section, sequence], norm_gain[section], query_weight[section], key_weight[section], value_weight[section], block_order[section, sequence], doc_ids[section, sequence]))
        section_outputs.append(jnp.stack(sequence_outputs))
    attended = jnp.stack(section_outputs)
    return jnp.roll(attended, 1, axis=0)
```

```python
import math

import jax
import jax.numpy as jnp
import numpy as np
from jax import lax
from jax.experimental import pallas as pl
from jax.experimental.pallas import tpu as pltpu
from jax.sharding import PartitionSpec as P

ROPE_BASE = 500000.0
EPSILON = 1e-05
FLOOR = -1e30
MASKED = -3e30
MESH = pl.DeviceIdType.MESH
F32 = jnp.float32
BF16 = jnp.bfloat16
RING = 8
HEAD = 128
BLOCK = 64


def rope_tables():
    freqs = ROPE_BASE ** (-np.arange(HEAD // 2, dtype=np.float64) * 2.0 / HEAD)
    coarse = np.arange(128, dtype=np.float64)[:, None] * BLOCK * freqs[None, :]
    fine = np.arange(BLOCK, dtype=np.float64)[:, None] * freqs[None, :]
    rows = [np.cos(coarse), np.sin(coarse), np.cos(fine), np.sin(fine)]
    table = np.concatenate(rows, axis=0)
    return np.concatenate([table, table], axis=1).astype(np.float32)


def wrap(i):
    return lax.rem(i + 2 * RING, RING)


class Gather:
    def __init__(self, bufs, rows, x, z, near_send, near_recv, far_send, far_recv):
        self.bufs, self.rows = bufs, rows
        self.small = (x, z)
        self.big = (z, x)
        self.near_send, self.near_recv = near_send, near_recv
        self.far_send, self.far_recv = far_send, far_recv
        self.x, self.z = x, z

    def small_device(self, half, by):
        if half == 0:
            return {"ctx": self.z * RING + wrap(self.x + by)}
        return {"ctx": wrap(self.z + by) * RING + self.x}

    def big_device(self, half, by):
        return self.small_device(1 - half, by)

    def slots(self, half, big, small, count):
        start = pl.multiple_of((big * RING + small) * self.rows, self.rows)
        return self.bufs[half].at[pl.ds(start, count * self.rows), :]

    def near(self, half, way, step, small):
        ref = self.slots(half, self.big[half], small, 1)
        return pltpu.make_async_remote_copy(
            src_ref=ref, dst_ref=ref,
            send_sem=self.near_send.at[half, way, step - 1],
            recv_sem=self.near_recv.at[half, way, step - 1],
            device_id=self.small_device(half, 1 - 2 * way), device_id_type=MESH)

    def far(self, half, way, hop, part, big, small, count):
        ref = self.slots(half, big, small, count)
        return pltpu.make_async_remote_copy(
            src_ref=ref, dst_ref=ref,
            send_sem=self.far_send.at[half, way, hop - 1, part],
            recv_sem=self.far_recv.at[half, way, hop - 1, part],
            device_id=self.big_device(half, 1 - 2 * way), device_id_type=MESH)

    def first_hop(self, half, small):
        for way in range(2):
            self.far(half, way, 1, small // 4, self.big[half], small, 1).start()

    def begin(self):
        for half in range(2):
            for way in range(2):
                self.near(half, way, 1, self.small[half]).start()
            self.first_hop(half, self.small[half])

    def near_steps(self):
        for step in range(1, 5):
            for half in range(2):
                for way in range(2):
                    if step == 4 and way == 1:
                        continue
                    came = wrap(self.small[half] - step * (1 - 2 * way))
                    self.near(half, way, step, came).wait_recv()
                    if step < 4 - way:
                        self.near(half, way, step + 1, came).start()
                    self.first_hop(half, came)

    def arrive_and_forward(self, hop, part):
        for half in range(2):
            for way in range(2):
                row = wrap(self.big[half] - hop * (1 - 2 * way))
                self.far(half, way, hop, part, row, part * 4, 4).wait_recv()

                @pl.when((hop < 3) | (part == way))
                def _():
                    self.far(half, way, hop + 1, part, row, part * 4, 4).start()

    def arrive_last(self):
        for half in range(2):
            for way in range(2):
                row = wrap(self.big[half] + 4)
                self.far(half, way, 4, way, row, way * 4, 4).wait_recv()

    def finish(self):
        for half in range(2):
            for way in range(2):
                for step in range(1, 5 - way):
                    self.near(half, way, step, self.small[half]).wait_send()
                for hop in range(1, 4):
                    for part in range(2):
                        self.far(half, way, hop, part, self.big[half], part * 4, 4).wait_send()
                self.far(half, way, 4, way, self.big[half], way * 4, 4).wait_send()


def kernel(tok_hbm, gain_ref, wq_hbm, wk_hbm, wv_hbm, order_ref, doc_ref, table_ref, out_ref,
           tok, normed, other, wq, wk, wv, w0, w1, part, kv_out, q_out, kv_in, q_in,
           kv0, kv1, meta_out, meta_in, meta_s, q_ref, qpos, qlo, run_max, acc, bias,
           load_sem, meta_sem, seed_send, seed_recv, tok_send, tok_recv, part_send, part_recv,
           w_ns, w_nr, w_fs, w_fr, kv_ns, kv_nr, kv_fs, kv_fr):
    ctx, y, section = lax.axis_index("ctx"), lax.axis_index("dp"), lax.axis_index("section")
    x, z = lax.rem(ctx, RING), ctx // RING
    mate = y + 1 - 2 * lax.rem(y, 2)
    twin = lax.rem(y + 2, 4)
    after, before = lax.rem(section + 1, 4), lax.rem(section + 3, 4)

    loads = [
        pltpu.make_async_copy(tok_hbm.at[0, 0], tok, load_sem.at[0]),
        pltpu.make_async_copy(wq_hbm.at[0], wq, load_sem.at[1]),
        pltpu.make_async_copy(wk_hbm.at[0], wk, load_sem.at[2]),
        pltpu.make_async_copy(wv_hbm.at[0], wv, load_sem.at[3]),
    ]
    for load in loads:
        load.start()

    weights = Gather((w0, w1), 16, x, z, w_ns, w_nr, w_fs, w_fr)
    kvs = Gather((kv0, kv1), BLOCK, x, z, kv_ns, kv_nr, kv_fs, kv_fr)

    barrier = pltpu.get_barrier_semaphore()
    greeted = [weights.small_device(half, by) for half in range(2) for by in (1, -1)]
    greeted += [{"dp": mate}, {"dp": twin}]
    greeted += [{"section": before}, {"section": before, "dp": mate}]
    for device in greeted:
        pl.semaphore_signal(barrier, inc=1, device_id=device, device_id_type=MESH)
    pl.semaphore_wait(barrier, len(greeted))

    rows0 = pl.ds(pl.multiple_of((z * RING + x) * 16, 16), 16)
    rows1 = pl.ds(pl.multiple_of((x * RING + z) * 16, 16), 16)

    def seed(number, src, dst):
        return pltpu.make_async_remote_copy(
            src_ref=src, dst_ref=dst, send_sem=seed_send.at[number],
            recv_sem=seed_recv.at[number], device_id={"dp": twin}, device_id_type=MESH)

    seeds = [
        seed(0, wq_hbm.at[0, rows0, pl.ds(0, 384)], w0.at[rows0, :]),
        seed(1, wq_hbm.at[0, rows1, pl.ds(384, 128)], w1.at[rows1, pl.ds(0, 128)]),
        seed(2, wk_hbm.at[0, rows1, :], w1.at[rows1, pl.ds(128, 128)]),
        seed(3, wv_hbm.at[0, rows1, :], w1.at[rows1, pl.ds(256, 128)]),
    ]
    for copy in seeds:
        copy.start()

    meta_out[...] = jnp.zeros_like(meta_out)
    meta_out[0:1, :] = order_ref[...]
    documents = doc_ref[...]
    for number in range(1, 4):
        count = jnp.sum(jnp.where(documents < number, 1.0, 0.0), axis=1, keepdims=True)
        meta_out[number:number + 1, :] = jnp.broadcast_to(count, (1, 128)).astype(jnp.int32)
    meta_copy = pltpu.make_async_remote_copy(
        src_ref=meta_out, dst_ref=meta_in, send_sem=meta_sem.at[0], recv_sem=meta_sem.at[1],
        device_id={"section": after}, device_id_type=MESH)
    meta_copy.start()

    loads[0].wait()
    wide = tok.shape[1] // 4
    square = jnp.zeros((128, 128), F32)
    for column in range(0, tok.shape[1], 128):
        piece = tok[:, column:column + 128].astype(F32)
        square = square + piece * piece
    mean = jnp.sum(square, axis=1, keepdims=True) * (1.0 / tok.shape[1])
    scale = lax.rsqrt(mean + EPSILON)

    def quarter(number):
        columns = pl.ds(pl.multiple_of(number * wide, wide), wide)
        value = tok[:, columns].astype(F32) * scale * gain_ref[:, columns]
        normed[number] = value.astype(BF16)

    def token_copy(slot, number):
        return pltpu.make_async_remote_copy(
            src_ref=normed.at[number], dst_ref=other.at[slot], send_sem=tok_send.at[slot],
            recv_sem=tok_recv.at[slot], device_id={"dp": mate}, device_id_type=MESH)

    token_copies = [token_copy(0, mate), token_copy(1, 3 - y)]
    quarter(mate)
    token_copies[0].start()
    quarter(3 - y)
    token_copies[1].start()

    for copy in seeds:
        copy.wait_recv()
    weights.begin()
    quarter(y)
    quarter(twin)
    weights.near_steps()

    for load in loads[1:]:
        load.wait()

    def own_rows(who, value):
        part[who, :, 0:512] = jnp.dot(value, wq[...], preferred_element_type=F32)
        part[who, :, 512:640] = jnp.dot(value, wk[...], preferred_element_type=F32)
        part[who, :, 640:768] = jnp.dot(value, wv[...], preferred_element_type=F32)

    def forward_step(t, carry):
        weights.arrive_and_forward(t // 2 + 1, lax.rem(t, 2))
        return carry

    own_rows(0, normed[y])
    lax.fori_loop(0, 3, forward_step, 0)
    token_copies[0].wait_recv()
    own_rows(1, other[0])
    lax.fori_loop(3, 6, forward_step, 0)
    token_copies[1].wait_recv()
    weights.arrive_last()

    def part_copy(number, who, src, dst):
        device = {"section": after} if who == 0 else {"section": after, "dp": mate}
        return pltpu.make_async_remote_copy(
            src_ref=src.at[who], dst_ref=dst.at[who], send_sem=part_send.at[number],
            recv_sem=part_recv.at[number], device_id=device, device_id_type=MESH)

    part_copies = [part_copy(who, who, kv_out, kv_in) for who in range(2)]
    part_copies += [part_copy(2 + who, who, q_out, q_in) for who in range(2)]
    for who in (1, 0):
        value = normed[twin] if who == 0 else other[1]
        rest = jnp.dot(value, w1[...], preferred_element_type=F32)
        kv_out[who] = (part[who, :, 512:768] + rest[:, 128:384]).astype(BF16)
        part_copies[who].start()
        q_out[who, :, 384:512] = (part[who, :, 384:512] + rest[:, 0:128]).astype(BF16)
    for who in (1, 0):
        value = normed[twin] if who == 0 else other[1]
        rest = jnp.dot(value, w0[...], preferred_element_type=F32)
        q_out[who, :, 0:384] = (part[who, :, 0:384] + rest).astype(BF16)
        part_copies[2 + who].start()

    meta_copy.wait_recv()
    to_scalars = pltpu.make_async_copy(meta_in, meta_s, load_sem.at[4])
    to_scalars.start()
    to_scalars.wait()

    def block_of(slot_z, slot_x, half):
        return meta_s[0, (slot_z * RING + slot_x) * 2 + half]

    lane = lax.broadcasted_iota(jnp.int32, (BLOCK, HEAD), 1)
    sign = jnp.where(lane < HEAD // 2, -1.0, 1.0)
    fine_cos = table_ref[256:320, :]
    fine_sin = table_ref[320:384, :]
    turns = []
    for half in range(2):
        block = block_of(z, x, half)
        coarse_cos = table_ref[pl.ds(block, 1), :]
        coarse_sin = table_ref[pl.ds(block + 128, 1), :]
        cosine = coarse_cos * fine_cos - coarse_sin * fine_sin
        sine = (coarse_sin * fine_cos + coarse_cos * fine_sin) * sign
        turns.append((cosine, sine))
        position = block * BLOCK + lax.broadcasted_iota(jnp.int32, (BLOCK, 128), 0)
        low = jnp.zeros((BLOCK, 128), jnp.int32)
        for number in range(1, 4):
            start = meta_in[number:number + 1, :]
            low = jnp.maximum(low, jnp.where(start <= position, start, 0))
        qpos[half * BLOCK:(half + 1) * BLOCK, :] = position
        qlo[half * BLOCK:(half + 1) * BLOCK, :] = low

    def turned(value, half):
        cosine, sine = turns[half]
        return value * cosine + pltpu.roll(value, HEAD // 2, 1) * sine

    for copy in part_copies[:2]:
        copy.wait_recv()
    for half in range(2):
        rows = slice(half * BLOCK, (half + 1) * BLOCK)
        both = kv_in[0, rows, :].astype(F32) + kv_in[1, rows, :].astype(F32)
        big, small = (z, x) if half == 0 else (x, z)
        slot = pl.ds(pl.multiple_of((big * RING + small) * BLOCK, BLOCK), BLOCK)
        buffer = kv0 if half == 0 else kv1
        buffer[slot, 0:128] = turned(both[:, 0:128], half).astype(BF16)
        buffer[slot, 128:256] = both[:, 128:256].astype(BF16)
    kvs.begin()

    run_max[...] = jnp.full(run_max.shape, FLOOR, F32)
    acc[...] = jnp.zeros_like(acc)
    kvs.near_steps()
    for copy in part_copies[2:]:
        copy.wait_recv()
    for half in range(2):
        rows = slice(half * BLOCK, (half + 1) * BLOCK)
        for head in range(4):
            columns = slice(head * HEAD, (head + 1) * HEAD)
            both = q_in[0, rows, columns].astype(F32) + q_in[1, rows, columns].astype(F32)
            q_ref[head, rows, :] = turned(both, half).astype(BF16)

    scaling = math.log2(math.e) * HEAD ** -0.5
    lanes = lax.broadcasted_iota(jnp.int32, (1, 128), 1)
    inner = lax.rem(lanes, BLOCK)
    first = lanes < BLOCK

    def tile(t, carry):
        hop = (t + 1) // 2
        one_row = (t == 0) | (t == 7)
        half_row = lax.rem(t + 1, 2)

        @pl.when((t > 0) & (t < 7))
        def _():
            kvs.arrive_and_forward(hop, half_row)

        @pl.when(t == 7)
        def _():
            kvs.arrive_last()

        keys, values = [], []
        for half in range(2):
            for way in range(2):
                big = wrap(kvs.big[half] - hop * (1 - 2 * way))
                small = 4 * jnp.where(one_row, way, half_row)
                begin = pl.multiple_of((big * RING + small) * BLOCK, 4 * BLOCK)
                buffer = kv0 if half == 0 else kv1
                both = buffer[pl.ds(begin, 4 * BLOCK), :]
                keys.append(both[:, 0:128])
                values.append(both[:, 128:256])
                for pair in range(2):
                    numbers = []
                    for k in range(2):
                        inside = small + 2 * pair + k
                        if half == 0:
                            numbers.append(block_of(big, inside, 0))
                        else:
                            numbers.append(block_of(inside, big, 1))
                    position = jnp.where(first, numbers[0], numbers[1]) * BLOCK + inner
                    column = (half * 2 + way) * 256 + pair * 128
                    allowed = (position <= qpos[...]) & (position >= qlo[...])
                    bias[:, column:column + 128] = jnp.where(allowed, 0.0, MASKED)
        key = jnp.concatenate(keys, axis=0)
        value = jnp.concatenate(values, axis=0)
        value = jnp.concatenate([value, jnp.ones_like(value)], axis=1)
        for head in range(4):
            scores = lax.dot_general(q_ref[head], key, (((1,), (1,)), ((), ())),
                                     preferred_element_type=F32)
            scores = scores * scaling + bias[...]
            old = run_max[head]
            new = jnp.maximum(old, jnp.max(scores, axis=1, keepdims=True))
            run_max[head] = new
            probs = jnp.exp2(scores - new[:, 0:1]).astype(BF16)
            factor = jnp.exp2(old - new)
            got = jnp.dot(probs, value, preferred_element_type=F32)
            acc[head, :, 0:128] = acc[head, :, 0:128] * factor + got[:, 0:128]
            acc[head, :, 128:256] = acc[head, :, 128:256] * factor + got[:, 128:256]
        return carry

    lax.fori_loop(0, 8, tile, 0)

    for head in range(4):
        result = acc[head, :, 0:128] / acc[head, :, 128:256]
        out_ref[:, head * HEAD:(head + 1) * HEAD] = result.astype(BF16)

    for copy in seeds:
        copy.wait_send()
    meta_copy.wait_send()
    for copy in token_copies + part_copies:
        copy.wait_send()
    weights.finish()
    kvs.finish()


def local(tokens, norm_gain, query_weight, key_weight, value_weight, block_order, doc_ids):
    width = tokens.shape[3]
    deep = width // 4
    table = jnp.asarray(rope_tables())
    anywhere = pl.BlockSpec(memory_space=pl.ANY)
    vmem = pl.BlockSpec(memory_space=pltpu.VMEM)
    dma = pltpu.SemaphoreType.DMA
    out = pl.pallas_call(
        kernel,
        out_shape=jax.ShapeDtypeStruct((128, 512), BF16),
        in_specs=[anywhere, vmem, anywhere, anywhere, anywhere, vmem, vmem, vmem],
        out_specs=vmem,
        scratch_shapes=[
            pltpu.VMEM((128, width), BF16),
            pltpu.VMEM((4, 128, deep), BF16),
            pltpu.VMEM((2, 128, deep), BF16),
            pltpu.VMEM((deep, 512), BF16),
            pltpu.VMEM((deep, 128), BF16),
            pltpu.VMEM((deep, 128), BF16),
            pltpu.VMEM((deep, 384), BF16),
            pltpu.VMEM((deep, 384), BF16),
            pltpu.VMEM((2, 128, 768), F32),
            pltpu.VMEM((2, 128, 256), BF16),
            pltpu.VMEM((2, 128, 512), BF16),
            pltpu.VMEM((2, 128, 256), BF16),
            pltpu.VMEM((2, 128, 512), BF16),
            pltpu.VMEM((64 * BLOCK, 256), BF16),
            pltpu.VMEM((64 * BLOCK, 256), BF16),
            pltpu.VMEM((8, 128), jnp.int32),
            pltpu.VMEM((8, 128), jnp.int32),
            pltpu.SMEM((8, 128), jnp.int32),
            pltpu.VMEM((4, 128, 128), BF16),
            pltpu.VMEM((128, 128), jnp.int32),
            pltpu.VMEM((128, 128), jnp.int32),
            pltpu.VMEM((4, 128, 128), F32),
            pltpu.VMEM((4, 128, 256), F32),
            pltpu.VMEM((128, 1024), F32),
            dma((5,)), dma((2,)), dma((4,)), dma((4,)), dma((2,)), dma((2,)), dma((4,)), dma((4,)),
            dma((2, 2, 4)), dma((2, 2, 4)), dma((2, 2, 4, 2)), dma((2, 2, 4, 2)),
            dma((2, 2, 4)), dma((2, 2, 4)), dma((2, 2, 4, 2)), dma((2, 2, 4, 2)),
        ],
        compiler_params=pltpu.CompilerParams(
            collective_id=0, has_side_effects=True, vmem_limit_bytes=40 * 1024 * 1024),
        name="relay_attention",
    )(tokens, norm_gain, query_weight, key_weight, value_weight, block_order[0], doc_ids[0], table)
    return out[None, None]


def solution(mesh):
    in_specs = (
        P("section", "dp", "ctx", None),
        P("section", None),
        P("section", "dp", None),
        P("section", "dp", None),
        P("section", "dp", None),
        P("section", "dp", None),
        P("section", "dp", None),
    )
    out_specs = P("section", "dp", "ctx", None)
    return jax.shard_map(local, mesh=mesh, in_specs=in_specs, out_specs=out_specs, check_vma=False)
```

```python
import math

import jax
import jax.numpy as jnp
import numpy as np
from jax import lax
from jax.experimental import pallas as pl
from jax.experimental.pallas import tpu as pltpu
from jax.sharding import PartitionSpec as P

ROPE_BASE = 500000.0
EPSILON = 1e-05
FLOOR = -1e30
MASKED = -3e30
MESH = pl.DeviceIdType.MESH
F32 = jnp.float32
BF16 = jnp.bfloat16
RING = 8
HEAD = 128
BLOCK = 64


def rope_tables():
    freqs = ROPE_BASE ** (-np.arange(HEAD // 2, dtype=np.float64) * 2.0 / HEAD)
    coarse = np.arange(128, dtype=np.float64)[:, None] * BLOCK * freqs[None, :]
    fine = np.arange(BLOCK, dtype=np.float64)[:, None] * freqs[None, :]
    rows = [np.cos(coarse), np.sin(coarse), np.cos(fine), np.sin(fine)]
    table = np.concatenate(rows, axis=0)
    return np.concatenate([table, table], axis=1).astype(np.float32)


def wrap(i):
    return lax.rem(i + 2 * RING, RING)


class Plane:
    def __init__(self, bufs, x, z, near_send, near_recv, far_send, far_recv):
        self.bufs = bufs
        self.small = (x, z)
        self.big = (z, x)
        self.near_send, self.near_recv = near_send, near_recv
        self.far_send, self.far_recv = far_send, far_recv
        self.x, self.z = x, z

    def small_device(self, half, by):
        if half == 0:
            return {"ctx": self.z * RING + wrap(self.x + by)}
        return {"ctx": wrap(self.z + by) * RING + self.x}

    def big_device(self, half, by):
        return self.small_device(1 - half, by)


class Spread(Plane):
    def rows(self, half, big, small, begin=0, count=64):
        start = (lax.rem(big, 4) * 4 + lax.rem(small, 4)) * 64 + begin
        return self.bufs[half].at[pl.ds(pl.multiple_of(start, 32), count), :]

    def near(self, half, number, small):
        big = self.big[half]
        if number < 2:
            ref = self.rows(half, big, small)
        else:
            ref = self.rows(half, big, small, 32 * (number - 2), 32)
        return pltpu.make_async_remote_copy(
            src_ref=ref, dst_ref=ref, send_sem=self.near_send.at[half, number],
            recv_sem=self.near_recv.at[half, number],
            device_id=self.small_device(half, (1, -1, 2, -2)[number]), device_id_type=MESH)

    def far(self, half, number, kind, big):
        small = wrap(self.small[half] + (0, -1, 1, 2)[kind])
        ref = self.rows(half, big, small)
        by = (1, -1, 2 if kind < 2 else -2)[number]
        return pltpu.make_async_remote_copy(
            src_ref=ref, dst_ref=ref, send_sem=self.far_send.at[half, number, kind],
            recv_sem=self.far_recv.at[half, number, kind],
            device_id=self.big_device(half, by), device_id_type=MESH)

    def far_sends(self, half, kind):
        for number in (2, 0, 1):
            self.far(half, number, kind, self.big[half]).start()

    def begin(self, half):
        for number in (2, 3, 0, 1):
            self.near(half, number, self.small[half]).start()
        self.far_sends(half, 0)

    def near_steps(self):
        for numbers, kind in (((0,), 1), ((1,), 2), ((2, 3), 3)):
            for half in (1, 0):
                for number in numbers:
                    came = wrap(self.small[half] + (-1, 1, 2, 2)[number])
                    self.near(half, number, came).wait_recv()
                self.far_sends(half, kind)

    def arrive(self, half):
        for kind in range(4):
            for number in range(3):
                row = wrap(self.big[half] + (-1, 1, 2)[number])
                self.far(half, number, kind, row).wait_recv()

    def finish(self):
        for half in range(2):
            for number in range(4):
                self.near(half, number, self.small[half]).wait_send()
            for kind in range(4):
                for number in range(3):
                    self.far(half, number, kind, self.big[half]).wait_send()


class Gather(Plane):
    def slots(self, half, big, index, count):
        start = pl.multiple_of((big * RING + index) * BLOCK, BLOCK)
        return self.bufs[half].at[pl.ds(start, count * BLOCK), :]

    def came(self, way, step):
        return 2 * step - 1 + way if step else 0

    def near(self, half, way, step):
        jump = step if step < 3 else 1
        held = self.came(way, step - 1) if step > 2 else 0
        return pltpu.make_async_remote_copy(
            src_ref=self.slots(half, self.big[half], held, 1),
            dst_ref=self.slots(half, self.big[half], self.came(way, step), 1),
            send_sem=self.near_send.at[half, way, step - 1],
            recv_sem=self.near_recv.at[half, way, step - 1],
            device_id=self.small_device(half, jump * (1 - 2 * way)), device_id_type=MESH)

    def far(self, half, way, hop, part, big, index, count):
        ref = self.slots(half, big, index, count)
        return pltpu.make_async_remote_copy(
            src_ref=ref, dst_ref=ref,
            send_sem=self.far_send.at[half, way, hop - 1, part],
            recv_sem=self.far_recv.at[half, way, hop - 1, part],
            device_id=self.big_device(half, 1 - 2 * way), device_id_type=MESH)

    def first_hop(self, half, index):
        for way in range(2):
            self.far(half, way, 1, index // 2, self.big[half], index, 1).start()

    def begin(self, half):
        for step in range(1, 3):
            for way in range(2):
                self.near(half, way, step).start()
            if step == 1:
                self.first_hop(half, 0)

    def near_step(self, step):
        for half in range(2):
            for way in range(2):
                if step + way < 5:
                    self.near(half, way, step).wait_recv()
                    if step in (2, 3) and step + 1 + way < 5:
                        self.near(half, way, step + 1).start()
                    self.first_hop(half, self.came(way, step))

    def arrive(self, hop, part):
        for half in range(2):
            for way in range(2):
                if hop == 4 and part // 2 != way:
                    continue
                row = wrap(self.big[half] - hop * (1 - 2 * way))
                self.far(half, way, hop, part, row, part * 2, 2).wait_recv()
                if hop < 3 or (hop == 3 and part // 2 == way):
                    self.far(half, way, hop + 1, part, row, part * 2, 2).start()

    def finish(self):
        for half in range(2):
            for way in range(2):
                for step in range(1, 5 - way):
                    self.near(half, way, step).wait_send()
                for hop in range(1, 5):
                    for part in range(4):
                        if hop < 4 or part // 2 == way:
                            self.far(half, way, hop, part, self.big[half], part * 2, 2).wait_send()


def kernel(tok_hbm, gain_hbm, wq_hbm, wk_hbm, wv_hbm, order_hbm, doc_hbm, table_hbm, out_ref,
           gain_ref, order_ref, doc_ref, table_ref, tok, normed, other, wq, wk, wv, w0, w1, part, kv_out, q_out, kv_in, q_in,
           kv0, kv1, meta_out, meta_in, meta_s, q_ref, qpos, qlo, run_max, acc, bias,
           load_sem, meta_sem, seed_send, seed_recv, tok_send, tok_recv, part_send, part_recv,
           w_ns, w_nr, w_fs, w_fr, kv_ns, kv_nr, kv_fs, kv_fr):
    ctx, y, section = lax.axis_index("ctx"), lax.axis_index("dp"), lax.axis_index("section")
    x, z = lax.rem(ctx, RING), ctx // RING
    mate = y + 1 - 2 * lax.rem(y, 2)
    twin = lax.rem(y + 2, 4)
    after, before = lax.rem(section + 1, 4), lax.rem(section + 3, 4)

    small_loads = [
        pltpu.make_async_copy(order_hbm.at[0], order_ref, load_sem.at[5]),
        pltpu.make_async_copy(doc_hbm.at[0], doc_ref, load_sem.at[6]),
        pltpu.make_async_copy(gain_hbm, gain_ref, load_sem.at[7]),
        pltpu.make_async_copy(table_hbm, table_ref, load_sem.at[8]),
    ]
    loads = [
        pltpu.make_async_copy(tok_hbm.at[0, 0], tok, load_sem.at[0]),
        pltpu.make_async_copy(wq_hbm.at[0], wq, load_sem.at[1]),
        pltpu.make_async_copy(wk_hbm.at[0], wk, load_sem.at[2]),
        pltpu.make_async_copy(wv_hbm.at[0], wv, load_sem.at[3]),
    ]
    for load in loads[:1] + small_loads + loads[1:]:
        load.start()

    weights = Spread((w0, w1), x, z, w_ns, w_nr, w_fs, w_fr)
    kvs = Gather((kv0, kv1), x, z, kv_ns, kv_nr, kv_fs, kv_fr)

    barrier = pltpu.get_barrier_semaphore()
    greeted = [weights.small_device(half, by) for half in range(2)
               for by in (1, -1, 2, -2)]
    greeted += [{"dp": mate}, {"dp": twin}]
    greeted += [{"section": before}, {"section": before, "dp": mate}]
    for device in greeted:
        pl.semaphore_signal(barrier, inc=1, device_id=device, device_id_type=MESH)

    rows0 = pl.ds(pl.multiple_of((lax.rem(z, 4) * 4 + lax.rem(x, 4)) * 64, 64), 64)
    rows1 = pl.ds(pl.multiple_of((lax.rem(x, 4) * 4 + lax.rem(z, 4)) * 64, 64), 64)

    def seed(number, src, dst):
        return pltpu.make_async_remote_copy(
            src_ref=src, dst_ref=dst, send_sem=seed_send.at[number],
            recv_sem=seed_recv.at[number], device_id={"dp": twin}, device_id_type=MESH)

    seeds = [
        seed(0, wq_hbm.at[0, rows0, pl.ds(0, 384)], w0.at[rows0, :]),
        seed(1, wq_hbm.at[0, rows1, pl.ds(384, 128)], w1.at[rows1, pl.ds(0, 128)]),
        seed(2, wk_hbm.at[0, rows1, :], w1.at[rows1, pl.ds(128, 128)]),
        seed(3, wv_hbm.at[0, rows1, :], w1.at[rows1, pl.ds(256, 128)]),
    ]

    meta_out[...] = jnp.zeros_like(meta_out)
    small_loads[0].wait()
    small_loads[1].wait()
    meta_out[0:1, :] = order_ref[...]
    documents = doc_ref[...]
    for number in range(1, 4):
        count = jnp.sum(jnp.where(documents < number, 1.0, 0.0), axis=1, keepdims=True)
        meta_out[number:number + 1, :] = jnp.broadcast_to(count, (1, 128)).astype(jnp.int32)
    meta_copy = pltpu.make_async_remote_copy(
        src_ref=meta_out, dst_ref=meta_in, send_sem=meta_sem.at[0], recv_sem=meta_sem.at[1],
        device_id={"section": after}, device_id_type=MESH)

    loads[0].wait()
    small_loads[2].wait()
    wide = tok.shape[1] // 4
    square = jnp.zeros((128, 128), F32)
    for column in range(0, tok.shape[1], 128):
        piece = tok[:, column:column + 128].astype(F32)
        square = square + piece * piece
    mean = jnp.sum(square, axis=1, keepdims=True) * (1.0 / tok.shape[1])
    scale = lax.rsqrt(mean + EPSILON)

    def quarter(number):
        columns = pl.ds(pl.multiple_of(number * wide, wide), wide)
        value = tok[:, columns].astype(F32) * scale * gain_ref[:, columns]
        normed[number] = value.astype(BF16)

    def token_copy(slot, number):
        return pltpu.make_async_remote_copy(
            src_ref=normed.at[number], dst_ref=other.at[slot], send_sem=tok_send.at[slot],
            recv_sem=tok_recv.at[slot], device_id={"dp": mate}, device_id_type=MESH)

    token_copies = [token_copy(0, mate), token_copy(1, 3 - y)]
    quarter(mate)
    quarter(3 - y)

    pl.semaphore_wait(barrier, len(greeted))
    for copy in seeds[1:] + seeds[:1] + token_copies + [meta_copy]:
        copy.start()
    quarter(y)
    quarter(twin)
    for load in loads[1:]:
        load.wait()

    def own_rows(who, value):
        part[who, :, 0:512] = jnp.dot(value, wq[...], preferred_element_type=F32)
        part[who, :, 512:640] = jnp.dot(value, wk[...], preferred_element_type=F32)
        part[who, :, 640:768] = jnp.dot(value, wv[...], preferred_element_type=F32)

    own_rows(0, normed[y])
    for copy in seeds[1:]:
        copy.wait_recv()
    weights.begin(1)
    seeds[0].wait_recv()
    weights.begin(0)
    weights.near_steps()
    token_copies[0].wait_recv()
    own_rows(1, other[0])
    token_copies[1].wait_recv()
    weights.arrive(1)

    def part_copy(number, who, src, dst):
        device = {"section": after} if who == 0 else {"section": after, "dp": mate}
        return pltpu.make_async_remote_copy(
            src_ref=src.at[who], dst_ref=dst.at[who], send_sem=part_send.at[number],
            recv_sem=part_recv.at[number], device_id=device, device_id_type=MESH)

    part_copies = [part_copy(who, who, kv_out, kv_in) for who in range(2)]
    part_copies += [part_copy(2 + who, who, q_out, q_in) for who in range(2)]
    for who in (1, 0):
        value = normed[twin] if who == 0 else other[1]
        rest = jnp.dot(value, w1[...], preferred_element_type=F32)
        kv_out[who] = (part[who, :, 512:768] + rest[:, 128:384]).astype(BF16)
        part_copies[who].start()
        q_out[who, :, 384:512] = (part[who, :, 384:512] + rest[:, 0:128]).astype(BF16)
    weights.arrive(0)
    for who in (1, 0):
        value = normed[twin] if who == 0 else other[1]
        rest = jnp.dot(value, w0[...], preferred_element_type=F32)
        q_out[who, :, 0:384] = (part[who, :, 0:384] + rest).astype(BF16)
        part_copies[2 + who].start()

    meta_copy.wait_recv()
    small_loads[3].wait()
    to_scalars = pltpu.make_async_copy(meta_in, meta_s, load_sem.at[4])
    to_scalars.start()
    to_scalars.wait()

    def block_of(slot_z, slot_x, half):
        return meta_s[0, (slot_z * RING + slot_x) * 2 + half]

    lane = lax.broadcasted_iota(jnp.int32, (BLOCK, HEAD), 1)
    sign = jnp.where(lane < HEAD // 2, -1.0, 1.0)
    fine_cos = table_ref[256:320, :]
    fine_sin = table_ref[320:384, :]
    turns = []
    for half in range(2):
        block = block_of(z, x, half)
        coarse_cos = table_ref[pl.ds(block, 1), :]
        coarse_sin = table_ref[pl.ds(block + 128, 1), :]
        cosine = coarse_cos * fine_cos - coarse_sin * fine_sin
        sine = (coarse_sin * fine_cos + coarse_cos * fine_sin) * sign
        turns.append((cosine, sine))
        position = block * BLOCK + lax.broadcasted_iota(jnp.int32, (BLOCK, 128), 0)
        low = jnp.zeros((BLOCK, 128), jnp.int32)
        for number in range(1, 4):
            start = meta_in[number:number + 1, :]
            low = jnp.maximum(low, jnp.where(start <= position, start, 0))
        qpos[half * BLOCK:(half + 1) * BLOCK, :] = position
        qlo[half * BLOCK:(half + 1) * BLOCK, :] = low

    def turned(value, half):
        cosine, sine = turns[half]
        return value * cosine + pltpu.roll(value, HEAD // 2, 1) * sine

    for copy in part_copies[:2]:
        copy.wait_recv()
    for half in range(2):
        rows = slice(half * BLOCK, (half + 1) * BLOCK)
        both = kv_in[0, rows, :].astype(F32) + kv_in[1, rows, :].astype(F32)
        big = z if half == 0 else x
        slot = pl.ds(pl.multiple_of(big * RING * BLOCK, BLOCK), BLOCK)
        buffer = kv0 if half == 0 else kv1
        buffer[slot, 0:128] = turned(both[:, 0:128], half).astype(BF16)
        buffer[slot, 128:256] = both[:, 128:256].astype(BF16)
    kvs.begin(0)
    kvs.begin(1)

    run_max[...] = jnp.full(run_max.shape, FLOOR, F32)
    acc[...] = jnp.zeros_like(acc)
    kvs.near_step(1)
    kvs.near_step(2)
    kvs.arrive(1, 0)
    kvs.near_step(3)
    kvs.arrive(1, 1)
    kvs.arrive(2, 0)
    kvs.near_step(4)
    for copy in part_copies[2:]:
        copy.wait_recv()
    for half in range(2):
        rows = slice(half * BLOCK, (half + 1) * BLOCK)
        for head in range(4):
            columns = slice(head * HEAD, (head + 1) * HEAD)
            both = q_in[0, rows, columns].astype(F32) + q_in[1, rows, columns].astype(F32)
            q_ref[head, rows, :] = turned(both, half).astype(BF16)

    scaling = math.log2(math.e) * HEAD ** -0.5
    lanes = lax.broadcasted_iota(jnp.int32, (1, 128), 1)
    inner = lax.rem(lanes, BLOCK)
    first = lanes < BLOCK

    def tile(t, carry):
        one_row = (t == 0) | (t == 7)
        hop = jnp.where(t == 0, 0, jnp.where((t == 1) | (t == 3), 1, jnp.where(
            (t == 2) | (t == 5), 2, jnp.where(t == 7, 4, 3))))
        half_row = jnp.where((t == 3) | (t == 5) | (t == 6), 1, 0)
        due = {1: [(1, 2)], 2: [(2, 1), (3, 0), (1, 3)], 3: [(2, 2)], 4: [(3, 1), (2, 3)],
               5: [(3, 2)], 6: [(3, 3)], 7: [(4, 0), (4, 1), (4, 2), (4, 3)]}
        for number, pieces in due.items():
            @pl.when(t == number)
            def _(pieces=pieces):
                for piece in pieces:
                    kvs.arrive(*piece)

        keys, values = [], []
        for half in range(2):
            for way in range(2):
                big = wrap(kvs.big[half] - hop * (1 - 2 * way))
                small = 4 * jnp.where(one_row, way, half_row)
                begin = pl.multiple_of((big * RING + small) * BLOCK, 4 * BLOCK)
                buffer = kv0 if half == 0 else kv1
                both = buffer[pl.ds(begin, 4 * BLOCK), :]
                keys.append(both[:, 0:128])
                values.append(both[:, 128:256])
                for pair in range(2):
                    numbers = []
                    for k in range(2):
                        index = small + 2 * pair + k
                        offset = (index + 1) // 2 * (1 - 2 * lax.rem(index, 2))
                        inside = wrap(kvs.small[half] + offset)
                        if half == 0:
                            numbers.append(block_of(big, inside, 0))
                        else:
                            numbers.append(block_of(inside, big, 1))
                    position = jnp.where(first, numbers[0], numbers[1]) * BLOCK + inner
                    column = (half * 2 + way) * 256 + pair * 128
                    allowed = (position <= qpos[...]) & (position >= qlo[...])
                    bias[:, column:column + 128] = jnp.where(allowed, 0.0, MASKED)
        key = jnp.concatenate(keys, axis=0)
        value = jnp.concatenate(values, axis=0)
        value = jnp.concatenate([value, jnp.ones_like(value)], axis=1)
        for head in range(4):
            scores = lax.dot_general(q_ref[head], key, (((1,), (1,)), ((), ())),
                                     preferred_element_type=F32)
            scores = scores * scaling + bias[...]
            old = run_max[head]
            new = jnp.maximum(old, jnp.max(scores, axis=1, keepdims=True))
            run_max[head] = new
            probs = jnp.exp2(scores - new[:, 0:1]).astype(BF16)
            factor = jnp.exp2(old - new)
            got = jnp.dot(probs, value, preferred_element_type=F32)
            acc[head, :, 0:128] = acc[head, :, 0:128] * factor + got[:, 0:128]
            acc[head, :, 128:256] = acc[head, :, 128:256] * factor + got[:, 128:256]
        return carry

    lax.fori_loop(0, 8, tile, 0)

    for head in range(4):
        result = acc[head, :, 0:128] / acc[head, :, 128:256]
        out_ref[:, head * HEAD:(head + 1) * HEAD] = result.astype(BF16)

    for copy in seeds:
        copy.wait_send()
    meta_copy.wait_send()
    for copy in token_copies + part_copies:
        copy.wait_send()
    weights.finish()
    kvs.finish()


def local(tokens, norm_gain, query_weight, key_weight, value_weight, block_order, doc_ids):
    width = tokens.shape[3]
    deep = width // 4
    table = jnp.asarray(rope_tables())
    hbm = pl.BlockSpec(memory_space=pltpu.HBM)
    vmem = pl.BlockSpec(memory_space=pltpu.VMEM)
    dma = pltpu.SemaphoreType.DMA
    out = pl.pallas_call(
        kernel,
        out_shape=jax.ShapeDtypeStruct((128, 512), BF16),
        in_specs=[hbm] * 8,
        out_specs=vmem,
        scratch_shapes=[
            pltpu.VMEM((1, width), F32),
            pltpu.VMEM((1, 128), jnp.int32),
            pltpu.VMEM((1, doc_ids.shape[2]), jnp.int32),
            pltpu.VMEM(table.shape, F32),
            pltpu.VMEM((128, width), BF16),
            pltpu.VMEM((4, 128, deep), BF16),
            pltpu.VMEM((2, 128, deep), BF16),
            pltpu.VMEM((deep, 512), BF16),
            pltpu.VMEM((deep, 128), BF16),
            pltpu.VMEM((deep, 128), BF16),
            pltpu.VMEM((deep, 384), BF16),
            pltpu.VMEM((deep, 384), BF16),
            pltpu.VMEM((2, 128, 768), F32),
            pltpu.VMEM((2, 128, 256), BF16),
            pltpu.VMEM((2, 128, 512), BF16),
            pltpu.VMEM((2, 128, 256), BF16),
            pltpu.VMEM((2, 128, 512), BF16),
            pltpu.VMEM((64 * BLOCK, 256), BF16),
            pltpu.VMEM((64 * BLOCK, 256), BF16),
            pltpu.VMEM((8, 128), jnp.int32),
            pltpu.VMEM((8, 128), jnp.int32),
            pltpu.SMEM((8, 128), jnp.int32),
            pltpu.VMEM((4, 128, 128), BF16),
            pltpu.VMEM((128, 128), jnp.int32),
            pltpu.VMEM((128, 128), jnp.int32),
            pltpu.VMEM((4, 128, 128), F32),
            pltpu.VMEM((4, 128, 256), F32),
            pltpu.VMEM((128, 1024), F32),
            dma((9,)), dma((2,)), dma((4,)), dma((4,)), dma((2,)), dma((2,)), dma((4,)), dma((4,)),
            dma((2, 4)), dma((2, 4)), dma((2, 3, 4)), dma((2, 3, 4)),
            dma((2, 2, 4)), dma((2, 2, 4)), dma((2, 2, 4, 4)), dma((2, 2, 4, 4)),
        ],
        compiler_params=pltpu.CompilerParams(
            collective_id=0, has_side_effects=True, vmem_limit_bytes=63 * 1024 * 1024),
        name="relay_attention",
    )(tokens, norm_gain, query_weight, key_weight, value_weight, block_order, doc_ids, table)
    return out[None, None]


def solution(mesh):
    in_specs = (
        P("section", "dp", "ctx", None),
        P("section", None),
        P("section", "dp", None),
        P("section", "dp", None),
        P("section", "dp", None),
        P("section", "dp", None),
        P("section", "dp", None),
    )
    out_specs = P("section", "dp", "ctx", None)
    return jax.shard_map(local, mesh=mesh, in_specs=in_specs, out_specs=out_specs, check_vma=False)
```

```python
import math

import jax
import jax.numpy as jnp
import numpy as np
from jax import lax
from jax.experimental import pallas as pl
from jax.experimental.pallas import tpu as pltpu
from jax.sharding import PartitionSpec as P

ROPE_BASE = 500000.0
EPSILON = 1e-05
FLOOR = -1e30
MASKED = -3e30
MESH = pl.DeviceIdType.MESH
F32 = jnp.float32
BF16 = jnp.bfloat16
RING = 8
HEAD = 128
BLOCK = 64


def rope_tables():
    freqs = ROPE_BASE ** (-np.arange(HEAD // 2, dtype=np.float64) * 2.0 / HEAD)
    coarse = np.arange(128, dtype=np.float64)[:, None] * BLOCK * freqs[None, :]
    fine = np.arange(BLOCK, dtype=np.float64)[:, None] * freqs[None, :]
    rows = [np.cos(coarse), np.sin(coarse), np.cos(fine), np.sin(fine)]
    table = np.concatenate(rows, axis=0)
    return np.concatenate([table, table], axis=1).astype(np.float32)


def wrap(i):
    return lax.rem(i + 2 * RING, RING)


class Plane:
    def __init__(self, bufs, x, z, near_send, near_recv, far_send, far_recv):
        self.bufs = bufs
        self.small = (x, z)
        self.big = (z, x)
        self.near_send, self.near_recv = near_send, near_recv
        self.far_send, self.far_recv = far_send, far_recv
        self.x, self.z = x, z

    def small_device(self, half, by):
        if half == 0:
            return {"ctx": self.z * RING + wrap(self.x + by)}
        return {"ctx": wrap(self.z + by) * RING + self.x}

    def big_device(self, half, by):
        return self.small_device(1 - half, by)


class Spread(Plane):
    def rows(self, half, big, small, begin=0, count=64):
        start = (lax.rem(big, 4) * 4 + lax.rem(small, 4)) * 64 + begin
        return self.bufs[half].at[pl.ds(pl.multiple_of(start, 32), count), :]

    def near(self, half, number, small):
        big = self.big[half]
        if number < 2:
            ref = self.rows(half, big, small)
        else:
            ref = self.rows(half, big, small, 32 * (number - 2), 32)
        return pltpu.make_async_remote_copy(
            src_ref=ref, dst_ref=ref, send_sem=self.near_send.at[half, number],
            recv_sem=self.near_recv.at[half, number],
            device_id=self.small_device(half, (1, -1, 2, -2)[number]), device_id_type=MESH)

    def far(self, half, number, kind, big):
        small = wrap(self.small[half] + (0, -1, 1, 2)[kind])
        ref = self.rows(half, big, small)
        by = (1, -1, 2 if kind < 2 else -2)[number]
        return pltpu.make_async_remote_copy(
            src_ref=ref, dst_ref=ref, send_sem=self.far_send.at[half, number, kind],
            recv_sem=self.far_recv.at[half, number, kind],
            device_id=self.big_device(half, by), device_id_type=MESH)

    def far_sends(self, half, kind):
        for number in (2, 0, 1):
            self.far(half, number, kind, self.big[half]).start()

    def begin(self, half):
        for number in (2, 3, 0, 1):
            self.near(half, number, self.small[half]).start()
        self.far_sends(half, 0)

    def near_steps(self):
        for numbers, kind in (((0,), 1), ((1,), 2), ((2, 3), 3)):
            for half in (1, 0):
                for number in numbers:
                    came = wrap(self.small[half] + (-1, 1, 2, 2)[number])
                    self.near(half, number, came).wait_recv()
                self.far_sends(half, kind)

    def arrive(self, half):
        for kind in range(4):
            for number in range(3):
                row = wrap(self.big[half] + (-1, 1, 2)[number])
                self.far(half, number, kind, row).wait_recv()

    def finish(self):
        for half in range(2):
            for number in range(4):
                self.near(half, number, self.small[half]).wait_send()
            for kind in range(4):
                for number in range(3):
                    self.far(half, number, kind, self.big[half]).wait_send()


class Gather(Plane):
    def slots(self, half, big, index, count):
        start = pl.multiple_of((big * RING + index) * BLOCK, BLOCK)
        return self.bufs[half].at[pl.ds(start, count * BLOCK), :]

    def came(self, way, step):
        return 2 * step - 1 + way if step else 0

    def near(self, half, way, step):
        jump = step if step < 3 else 1
        held = self.came(way, step - 1) if step > 2 else 0
        return pltpu.make_async_remote_copy(
            src_ref=self.slots(half, self.big[half], held, 1),
            dst_ref=self.slots(half, self.big[half], self.came(way, step), 1),
            send_sem=self.near_send.at[half, way, step - 1],
            recv_sem=self.near_recv.at[half, way, step - 1],
            device_id=self.small_device(half, jump * (1 - 2 * way)), device_id_type=MESH)

    def far(self, half, way, hop, part, big, index, count):
        ref = self.slots(half, big, index, count)
        return pltpu.make_async_remote_copy(
            src_ref=ref, dst_ref=ref,
            send_sem=self.far_send.at[half, way, hop - 1, part],
            recv_sem=self.far_recv.at[half, way, hop - 1, part],
            device_id=self.big_device(half, 1 - 2 * way), device_id_type=MESH)

    def first_hop(self, half, index):
        for way in range(2):
            self.far(half, way, 1, index // 2, self.big[half], index, 1).start()

    def begin(self, half):
        for step in range(1, 3):
            for way in range(2):
                self.near(half, way, step).start()
            if step == 1:
                self.first_hop(half, 0)

    def near_step(self, step):
        for half in range(2):
            for way in range(2):
                if step + way < 5:
                    self.near(half, way, step).wait_recv()
                    if step in (2, 3) and step + 1 + way < 5:
                        self.near(half, way, step + 1).start()
                    self.first_hop(half, self.came(way, step))

    def arrive(self, hop, part):
        for half in range(2):
            for way in range(2):
                if hop == 4 and part // 2 != way:
                    continue
                row = wrap(self.big[half] - hop * (1 - 2 * way))
                self.far(half, way, hop, part, row, part * 2, 2).wait_recv()
                if hop < 3 or (hop == 3 and part // 2 == way):
                    self.far(half, way, hop + 1, part, row, part * 2, 2).start()

    def drain(self, hops, near=False):
        for half in range(2):
            for way in range(2):
                for step in range(1, 5 - way if near else 1):
                    self.near(half, way, step).wait_send()
                for hop in hops:
                    for part in range(4):
                        if hop < 4 or part // 2 == way:
                            self.far(half, way, hop, part, self.big[half], part * 2, 2).wait_send()


def kernel(tok_hbm, gain_hbm, wq_hbm, wk_hbm, wv_hbm, order_hbm, doc_hbm, table_hbm, out_ref,
           gain_ref, order_ref, doc_ref, table_ref, tok, normed, other, wq, wk, wv, wk_g, wv_g, wq0_g, wq1_g, part, kv_out, q_out, kv_in, q_in,
           kv0, kv1, meta_out, meta_in, meta_s, q_ref, qpos, qlo, run_max, acc, bias,
           load_sem, meta_sem, seed_send, seed_recv, tok_send, tok_recv, part_send, part_recv,
           w_ns, w_nr, w_fs, w_fr, wq_ns, wq_nr, wq_fs, wq_fr, kv_ns, kv_nr, kv_fs, kv_fr):
    ctx, y, section = lax.axis_index("ctx"), lax.axis_index("dp"), lax.axis_index("section")
    x, z = lax.rem(ctx, RING), ctx // RING
    mate = y + 1 - 2 * lax.rem(y, 2)
    twin = lax.rem(y + 2, 4)
    after, before = lax.rem(section + 1, 4), lax.rem(section + 3, 4)

    small_loads = [
        pltpu.make_async_copy(order_hbm.at[0], order_ref, load_sem.at[5]),
        pltpu.make_async_copy(doc_hbm.at[0], doc_ref, load_sem.at[6]),
        pltpu.make_async_copy(gain_hbm, gain_ref, load_sem.at[7]),
        pltpu.make_async_copy(table_hbm, table_ref, load_sem.at[8]),
    ]
    loads = [
        pltpu.make_async_copy(tok_hbm.at[0, 0], tok, load_sem.at[0]),
        pltpu.make_async_copy(wq_hbm.at[0], wq, load_sem.at[1]),
        pltpu.make_async_copy(wk_hbm.at[0], wk, load_sem.at[2]),
        pltpu.make_async_copy(wv_hbm.at[0], wv, load_sem.at[3]),
    ]
    for load in loads[:1] + small_loads + loads[1:]:
        load.start()

    kv_weights = Spread((wk_g, wv_g), x, z, w_ns, w_nr, w_fs, w_fr)
    q_weights = Spread((wq0_g, wq1_g), x, z, wq_ns, wq_nr, wq_fs, wq_fr)
    kvs = Gather((kv0, kv1), x, z, kv_ns, kv_nr, kv_fs, kv_fr)

    barrier = pltpu.get_barrier_semaphore()
    greeted = [kvs.small_device(half, by) for half in range(2)
               for by in (1, -1, 2, -2)]
    greeted += [{"dp": mate}, {"dp": twin}]
    greeted += [{"section": before}, {"section": before, "dp": mate}]
    for device in greeted:
        pl.semaphore_signal(barrier, inc=1, device_id=device, device_id_type=MESH)

    rows0 = pl.ds(pl.multiple_of((lax.rem(z, 4) * 4 + lax.rem(x, 4)) * 64, 64), 64)
    rows1 = pl.ds(pl.multiple_of((lax.rem(x, 4) * 4 + lax.rem(z, 4)) * 64, 64), 64)

    def seed(number, src, dst):
        return pltpu.make_async_remote_copy(
            src_ref=src, dst_ref=dst, send_sem=seed_send.at[number],
            recv_sem=seed_recv.at[number], device_id={"dp": twin}, device_id_type=MESH)

    seeds = [
        seed(0, wk_hbm.at[0, rows0, :], wk_g.at[rows0, :]),
        seed(1, wv_hbm.at[0, rows1, :], wv_g.at[rows1, :]),
        seed(2, wq_hbm.at[0, rows0, pl.ds(0, 256)], wq0_g.at[rows0, :]),
        seed(3, wq_hbm.at[0, rows1, pl.ds(256, 256)], wq1_g.at[rows1, :]),
    ]

    meta_out[...] = jnp.zeros_like(meta_out)
    small_loads[0].wait()
    small_loads[1].wait()
    meta_out[0:1, :] = order_ref[...]
    documents = doc_ref[...]
    for number in range(1, 4):
        count = jnp.sum(jnp.where(documents < number, 1.0, 0.0), axis=1, keepdims=True)
        meta_out[number:number + 1, :] = jnp.broadcast_to(count, (1, 128)).astype(jnp.int32)
    meta_copy = pltpu.make_async_remote_copy(
        src_ref=meta_out, dst_ref=meta_in, send_sem=meta_sem.at[0], recv_sem=meta_sem.at[1],
        device_id={"section": after}, device_id_type=MESH)

    loads[0].wait()
    small_loads[2].wait()
    wide = tok.shape[1] // 4
    square = jnp.zeros((128, 128), F32)
    for column in range(0, tok.shape[1], 128):
        piece = tok[:, column:column + 128].astype(F32)
        square = square + piece * piece
    mean = jnp.sum(square, axis=1, keepdims=True) * (1.0 / tok.shape[1])
    scale = lax.rsqrt(mean + EPSILON)

    def quarter(number):
        columns = pl.ds(pl.multiple_of(number * wide, wide), wide)
        value = tok[:, columns].astype(F32) * scale * gain_ref[:, columns]
        normed[number] = value.astype(BF16)

    def token_copy(slot, number):
        return pltpu.make_async_remote_copy(
            src_ref=normed.at[number], dst_ref=other.at[slot], send_sem=tok_send.at[slot],
            recv_sem=tok_recv.at[slot], device_id={"dp": mate}, device_id_type=MESH)

    token_copies = [token_copy(0, mate), token_copy(1, 3 - y)]
    quarter(mate)
    quarter(3 - y)

    pl.semaphore_wait(barrier, len(greeted))
    for copy in seeds + token_copies + [meta_copy]:
        copy.start()
    quarter(y)
    quarter(twin)
    for load in loads[1:]:
        load.wait()

    def own_rows(who, value):
        part[who, :, 0:512] = jnp.dot(value, wq[...], preferred_element_type=F32)
        part[who, :, 512:640] = jnp.dot(value, wk[...], preferred_element_type=F32)
        part[who, :, 640:768] = jnp.dot(value, wv[...], preferred_element_type=F32)

    own_rows(0, normed[y])
    for number in range(4):
        seeds[number].wait_recv()
        (kv_weights, q_weights)[number // 2].begin(number % 2)
    kv_weights.near_steps()
    q_weights.near_steps()
    token_copies[0].wait_recv()
    own_rows(1, other[0])
    kv_weights.arrive(0)
    kv_weights.arrive(1)
    token_copies[1].wait_recv()

    def part_copy(number, who, src, dst):
        device = {"section": after} if who == 0 else {"section": after, "dp": mate}
        return pltpu.make_async_remote_copy(
            src_ref=src.at[who], dst_ref=dst.at[who], send_sem=part_send.at[number],
            recv_sem=part_recv.at[number], device_id=device, device_id_type=MESH)

    part_copies = [part_copy(who, who, kv_out, kv_in) for who in range(2)]
    part_copies += [part_copy(2 + who, who, q_out, q_in) for who in range(2)]
    for who in (1, 0):
        value = normed[twin] if who == 0 else other[1]
        for number, weight in enumerate((wk_g, wv_g)):
            rest = jnp.dot(value, weight[...], preferred_element_type=F32)
            columns = slice(number * 128, (number + 1) * 128)
            kv_out[who, :, columns] = (part[who, :, 512 + number * 128:640 + number * 128] + rest).astype(BF16)
        part_copies[who].start()
    q_weights.arrive(0)
    q_weights.arrive(1)
    for who in (1, 0):
        value = normed[twin] if who == 0 else other[1]
        for number, weight in enumerate((wq0_g, wq1_g)):
            rest = jnp.dot(value, weight[...], preferred_element_type=F32)
            columns = slice(number * 256, (number + 1) * 256)
            q_out[who, :, columns] = (part[who, :, columns] + rest).astype(BF16)
        part_copies[2 + who].start()

    meta_copy.wait_recv()
    small_loads[3].wait()
    to_scalars = pltpu.make_async_copy(meta_in, meta_s, load_sem.at[4])
    to_scalars.start()
    to_scalars.wait()

    def block_of(slot_z, slot_x, half):
        return meta_s[0, (slot_z * RING + slot_x) * 2 + half]

    lane = lax.broadcasted_iota(jnp.int32, (BLOCK, HEAD), 1)
    sign = jnp.where(lane < HEAD // 2, -1.0, 1.0)
    fine_cos = table_ref[256:320, :]
    fine_sin = table_ref[320:384, :]
    turns = []
    for half in range(2):
        block = block_of(z, x, half)
        coarse_cos = table_ref[pl.ds(block, 1), :]
        coarse_sin = table_ref[pl.ds(block + 128, 1), :]
        cosine = coarse_cos * fine_cos - coarse_sin * fine_sin
        sine = (coarse_sin * fine_cos + coarse_cos * fine_sin) * sign
        turns.append((cosine, sine))
        position = block * BLOCK + lax.broadcasted_iota(jnp.int32, (BLOCK, 128), 0)
        low = jnp.zeros((BLOCK, 128), jnp.int32)
        for number in range(1, 4):
            start = meta_in[number:number + 1, :]
            low = jnp.maximum(low, jnp.where(start <= position, start, 0))
        qpos[half * BLOCK:(half + 1) * BLOCK, :] = position
        qlo[half * BLOCK:(half + 1) * BLOCK, :] = low

    def turned(value, half):
        cosine, sine = turns[half]
        return value * cosine + pltpu.roll(value, HEAD // 2, 1) * sine

    for copy in part_copies[:2]:
        copy.wait_recv()
    for half in range(2):
        rows = slice(half * BLOCK, (half + 1) * BLOCK)
        both = kv_in[0, rows, :].astype(F32) + kv_in[1, rows, :].astype(F32)
        big = z if half == 0 else x
        slot = pl.ds(pl.multiple_of(big * RING * BLOCK, BLOCK), BLOCK)
        buffer = kv0 if half == 0 else kv1
        buffer[slot, 0:128] = turned(both[:, 0:128], half).astype(BF16)
        buffer[slot, 128:256] = both[:, 128:256].astype(BF16)
    kvs.begin(0)
    kvs.begin(1)
    kv_weights.finish()
    q_weights.finish()
    for copy in seeds + token_copies + [meta_copy]:
        copy.wait_send()

    run_max[...] = jnp.full(run_max.shape, FLOOR, F32)
    acc[...] = jnp.zeros_like(acc)
    kvs.near_step(1)
    kvs.near_step(2)
    kvs.arrive(1, 0)
    kvs.near_step(3)
    kvs.arrive(1, 1)
    kvs.arrive(2, 0)
    kvs.near_step(4)
    for copy in part_copies[2:]:
        copy.wait_recv()
    for copy in part_copies:
        copy.wait_send()
    for half in range(2):
        rows = slice(half * BLOCK, (half + 1) * BLOCK)
        for head in range(4):
            columns = slice(head * HEAD, (head + 1) * HEAD)
            both = q_in[0, rows, columns].astype(F32) + q_in[1, rows, columns].astype(F32)
            q_ref[head, rows, :] = turned(both, half).astype(BF16)

    scaling = math.log2(math.e) * HEAD ** -0.5
    lanes = lax.broadcasted_iota(jnp.int32, (1, 128), 1)
    inner = lax.rem(lanes, BLOCK)
    first = lanes < BLOCK

    def tile(t, carry):
        one_row = (t == 0) | (t == 7)
        hop = jnp.where(t == 0, 0, jnp.where((t == 1) | (t == 3), 1, jnp.where(
            (t == 2) | (t == 5), 2, jnp.where(t == 7, 4, 3))))
        half_row = jnp.where((t == 3) | (t == 5) | (t == 6), 1, 0)
        due = {1: [(1, 2)], 2: [(2, 1), (3, 0), (1, 3)], 3: [(2, 2)], 4: [(3, 1), (2, 3)],
               5: [(3, 2)], 6: [(3, 3)], 7: [(4, 0), (4, 1), (4, 2), (4, 3)]}
        for number, pieces in due.items():
            @pl.when(t == number)
            def _(pieces=pieces, number=number):
                if number == 6:
                    kvs.drain((1, 2), near=True)
                if number == 7:
                    kvs.drain((3,))
                for piece in pieces:
                    kvs.arrive(*piece)

        keys, values = [], []
        for half in range(2):
            for way in range(2):
                big = wrap(kvs.big[half] - hop * (1 - 2 * way))
                small = 4 * jnp.where(one_row, way, half_row)
                begin = pl.multiple_of((big * RING + small) * BLOCK, 4 * BLOCK)
                buffer = kv0 if half == 0 else kv1
                both = buffer[pl.ds(begin, 4 * BLOCK), :]
                keys.append(both[:, 0:128])
                values.append(both[:, 128:256])
                for pair in range(2):
                    numbers = []
                    for k in range(2):
                        index = small + 2 * pair + k
                        offset = (index + 1) // 2 * (1 - 2 * lax.rem(index, 2))
                        inside = wrap(kvs.small[half] + offset)
                        if half == 0:
                            numbers.append(block_of(big, inside, 0))
                        else:
                            numbers.append(block_of(inside, big, 1))
                    position = jnp.where(first, numbers[0], numbers[1]) * BLOCK + inner
                    column = (half * 2 + way) * 256 + pair * 128
                    allowed = (position <= qpos[...]) & (position >= qlo[...])
                    bias[:, column:column + 128] = jnp.where(allowed, 0.0, MASKED)
        key = jnp.concatenate(keys, axis=0)
        value = jnp.concatenate(values, axis=0)
        value = jnp.concatenate([value, jnp.ones_like(value)], axis=1)
        for head in range(4):
            scores = lax.dot_general(q_ref[head], key, (((1,), (1,)), ((), ())),
                                     preferred_element_type=F32)
            scores = scores * scaling + bias[...]
            old = run_max[head]
            new = jnp.maximum(old, jnp.max(scores, axis=1, keepdims=True))
            run_max[head] = new
            probs = jnp.exp2(scores - new[:, 0:1]).astype(BF16)
            factor = jnp.exp2(old - new)
            got = jnp.dot(probs, value, preferred_element_type=F32)
            acc[head, :, 0:128] = acc[head, :, 0:128] * factor + got[:, 0:128]
            acc[head, :, 128:256] = acc[head, :, 128:256] * factor + got[:, 128:256]
        return carry

    lax.fori_loop(0, 8, tile, 0)

    for head in range(4):
        result = acc[head, :, 0:128] / acc[head, :, 128:256]
        out_ref[:, head * HEAD:(head + 1) * HEAD] = result.astype(BF16)

    kvs.drain((4,))


def local(tokens, norm_gain, query_weight, key_weight, value_weight, block_order, doc_ids):
    width = tokens.shape[3]
    deep = width // 4
    table = jnp.asarray(rope_tables())
    hbm = pl.BlockSpec(memory_space=pltpu.HBM)
    vmem = pl.BlockSpec(memory_space=pltpu.VMEM)
    dma = pltpu.SemaphoreType.DMA
    out = pl.pallas_call(
        kernel,
        out_shape=jax.ShapeDtypeStruct((128, 512), BF16),
        in_specs=[hbm] * 8,
        out_specs=vmem,
        scratch_shapes=[
            pltpu.VMEM((1, width), F32),
            pltpu.VMEM((1, 128), jnp.int32),
            pltpu.VMEM((1, doc_ids.shape[2]), jnp.int32),
            pltpu.VMEM(table.shape, F32),
            pltpu.VMEM((128, width), BF16),
            pltpu.VMEM((4, 128, deep), BF16),
            pltpu.VMEM((2, 128, deep), BF16),
            pltpu.VMEM((deep, 512), BF16),
            pltpu.VMEM((deep, 128), BF16),
            pltpu.VMEM((deep, 128), BF16),
            pltpu.VMEM((deep, 128), BF16),
            pltpu.VMEM((deep, 128), BF16),
            pltpu.VMEM((deep, 256), BF16),
            pltpu.VMEM((deep, 256), BF16),
            pltpu.VMEM((2, 128, 768), F32),
            pltpu.VMEM((2, 128, 256), BF16),
            pltpu.VMEM((2, 128, 512), BF16),
            pltpu.VMEM((2, 128, 256), BF16),
            pltpu.VMEM((2, 128, 512), BF16),
            pltpu.VMEM((64 * BLOCK, 256), BF16),
            pltpu.VMEM((64 * BLOCK, 256), BF16),
            pltpu.VMEM((8, 128), jnp.int32),
            pltpu.VMEM((8, 128), jnp.int32),
            pltpu.SMEM((8, 128), jnp.int32),
            pltpu.VMEM((4, 128, 128), BF16),
            pltpu.VMEM((128, 128), jnp.int32),
            pltpu.VMEM((128, 128), jnp.int32),
            pltpu.VMEM((4, 128, 128), F32),
            pltpu.VMEM((4, 128, 256), F32),
            pltpu.VMEM((128, 1024), F32),
            dma((9,)), dma((2,)), dma((4,)), dma((4,)), dma((2,)), dma((2,)), dma((4,)), dma((4,)),
            dma((2, 4)), dma((2, 4)), dma((2, 3, 4)), dma((2, 3, 4)),
            dma((2, 4)), dma((2, 4)), dma((2, 3, 4)), dma((2, 3, 4)),
            dma((2, 2, 4)), dma((2, 2, 4)), dma((2, 2, 4, 4)), dma((2, 2, 4, 4)),
        ],
        compiler_params=pltpu.CompilerParams(
            collective_id=0, has_side_effects=True, vmem_limit_bytes=63 * 1024 * 1024),
        name="relay_attention",
    )(tokens, norm_gain, query_weight, key_weight, value_weight, block_order, doc_ids, table)
    return out[None, None]


def solution(mesh):
    in_specs = (
        P("section", "dp", "ctx", None),
        P("section", None),
        P("section", "dp", None),
        P("section", "dp", None),
        P("section", "dp", None),
        P("section", "dp", None),
        P("section", "dp", None),
    )
    out_specs = P("section", "dp", "ctx", None)
    return jax.shard_map(local, mesh=mesh, in_specs=in_specs, out_specs=out_specs, check_vma=False)
```

```python
import math

import jax
import jax.numpy as jnp
import numpy as np
from jax import lax
from jax.experimental import pallas as pl
from jax.experimental.pallas import tpu as pltpu
from jax.sharding import PartitionSpec as P

ROPE_BASE = 500000.0
EPSILON = 1e-05
FLOOR = -1e30
MASKED = -3e30
MESH = pl.DeviceIdType.MESH
F32 = jnp.float32
BF16 = jnp.bfloat16
RING = 8
HEAD = 128
BLOCK = 64


def rope_tables():
    freqs = ROPE_BASE ** (-np.arange(HEAD // 2, dtype=np.float64) * 2.0 / HEAD)
    coarse = np.arange(128, dtype=np.float64)[:, None] * BLOCK * freqs[None, :]
    fine = np.arange(BLOCK, dtype=np.float64)[:, None] * freqs[None, :]
    rows = [np.cos(coarse), np.sin(coarse), np.cos(fine), np.sin(fine)]
    table = np.concatenate(rows, axis=0)
    return np.concatenate([table, table], axis=1).astype(np.float32)


def wrap(i):
    return lax.rem(i + 2 * RING, RING)


class Plane:
    def __init__(self, bufs, x, z, near_send, near_recv, far_send, far_recv):
        self.bufs = bufs
        self.small = (x, z)
        self.big = (z, x)
        self.near_send, self.near_recv = near_send, near_recv
        self.far_send, self.far_recv = far_send, far_recv
        self.x, self.z = x, z

    def small_device(self, half, by):
        if half == 0:
            return {"ctx": self.z * RING + wrap(self.x + by)}
        return {"ctx": wrap(self.z + by) * RING + self.x}

    def big_device(self, half, by):
        return self.small_device(1 - half, by)


class Spread(Plane):
    def rows(self, half, big, small, begin=0, count=64):
        start = (lax.rem(big, 4) * 4 + lax.rem(small, 4)) * 64 + begin
        return self.bufs[half].at[pl.ds(pl.multiple_of(start, 32), count), :]

    def near(self, half, number, small):
        big = self.big[half]
        if number < 2:
            ref = self.rows(half, big, small)
        else:
            ref = self.rows(half, big, small, 32 * (number - 2), 32)
        return pltpu.make_async_remote_copy(
            src_ref=ref, dst_ref=ref, send_sem=self.near_send.at[half, number],
            recv_sem=self.near_recv.at[half, number],
            device_id=self.small_device(half, (1, -1, 2, -2)[number]), device_id_type=MESH)

    def far(self, half, number, kind, big):
        small = wrap(self.small[half] + (0, -1, 1, 2)[kind])
        ref = self.rows(half, big, small)
        by = (1, -1, 2 if kind < 2 else -2)[number]
        return pltpu.make_async_remote_copy(
            src_ref=ref, dst_ref=ref, send_sem=self.far_send.at[half, number, kind],
            recv_sem=self.far_recv.at[half, number, kind],
            device_id=self.big_device(half, by), device_id_type=MESH)

    def far_sends(self, half, kind):
        for number in (2, 0, 1):
            self.far(half, number, kind, self.big[half]).start()

    def begin(self, half):
        for number in (2, 3, 0, 1):
            self.near(half, number, self.small[half]).start()
        self.far_sends(half, 0)

    def near_steps(self):
        for numbers, kind in (((0,), 1), ((1,), 2), ((2, 3), 3)):
            for half in (1, 0):
                for number in numbers:
                    came = wrap(self.small[half] + (-1, 1, 2, 2)[number])
                    self.near(half, number, came).wait_recv()
                self.far_sends(half, kind)

    def arrive(self, half):
        for kind in range(4):
            for number in range(3):
                row = wrap(self.big[half] + (-1, 1, 2)[number])
                self.far(half, number, kind, row).wait_recv()

    def finish(self):
        for half in range(2):
            for number in range(4):
                self.near(half, number, self.small[half]).wait_send()
            for kind in range(4):
                for number in range(3):
                    self.far(half, number, kind, self.big[half]).wait_send()


class Gather(Plane):
    def slots(self, half, big, index, count):
        start = pl.multiple_of((big * RING + index) * BLOCK, BLOCK)
        return self.bufs[half].at[pl.ds(start, count * BLOCK), :]

    def came(self, way, step):
        return 2 * step - 1 + way if step else 0

    def near(self, half, way, step):
        jump = step if step < 3 else 1
        held = self.came(way, step - 1) if step > 2 else 0
        return pltpu.make_async_remote_copy(
            src_ref=self.slots(half, self.big[half], held, 1),
            dst_ref=self.slots(half, self.big[half], self.came(way, step), 1),
            send_sem=self.near_send.at[half, way, step - 1],
            recv_sem=self.near_recv.at[half, way, step - 1],
            device_id=self.small_device(half, jump * (1 - 2 * way)), device_id_type=MESH)

    def far(self, half, way, hop, part, big, index, count):
        ref = self.slots(half, big, index, count)
        return pltpu.make_async_remote_copy(
            src_ref=ref, dst_ref=ref,
            send_sem=self.far_send.at[half, way, hop - 1, part],
            recv_sem=self.far_recv.at[half, way, hop - 1, part],
            device_id=self.big_device(half, 1 - 2 * way), device_id_type=MESH)

    def first_hop(self, half, index):
        for way in range(2):
            self.far(half, way, 1, index // 2, self.big[half], index, 1).start()

    def begin(self, half):
        for step in range(1, 3):
            for way in range(2):
                self.near(half, way, step).start()
            if step == 1:
                self.first_hop(half, 0)

    def near_step(self, step):
        for half in range(2):
            for way in range(2):
                if step + way < 5:
                    self.near(half, way, step).wait_recv()
                    if step in (2, 3) and step + 1 + way < 5:
                        self.near(half, way, step + 1).start()
                    self.first_hop(half, self.came(way, step))

    def arrive(self, hop, part):
        for half in range(2):
            for way in range(2):
                if hop == 4 and part // 2 != way:
                    continue
                row = wrap(self.big[half] - hop * (1 - 2 * way))
                self.far(half, way, hop, part, row, part * 2, 2).wait_recv()
                if hop < 3 or (hop == 3 and part // 2 == way):
                    self.far(half, way, hop + 1, part, row, part * 2, 2).start()

    def drain(self, hops, near=False):
        for half in range(2):
            for way in range(2):
                for step in range(1, 5 - way if near else 1):
                    self.near(half, way, step).wait_send()
                for hop in hops:
                    for part in range(4):
                        if hop < 4 or part // 2 == way:
                            self.far(half, way, hop, part, self.big[half], part * 2, 2).wait_send()


def kernel(tok_hbm, gain_hbm, wq_hbm, wk_hbm, wv_hbm, order_hbm, doc_hbm, table_hbm, out_ref,
           gain_ref, order_ref, doc_ref, table_ref, tok, normed, other, wq, wk, wv, wk_g, wv_g, wq0_g, wq1_g, part, kv_out, q_out, kv_in, q_in,
           kv0, kv1, meta_out, meta_in, meta_s, q_ref, qpos, qlo, run_max, acc, bias,
           load_sem, meta_sem, seed_send, seed_recv, tok_send, tok_recv, part_send, part_recv,
           w_ns, w_nr, w_fs, w_fr, wq_ns, wq_nr, wq_fs, wq_fr, kv_ns, kv_nr, kv_fs, kv_fr):
    ctx, y, section = lax.axis_index("ctx"), lax.axis_index("dp"), lax.axis_index("section")
    x, z = lax.rem(ctx, RING), ctx // RING
    mate = y + 1 - 2 * lax.rem(y, 2)
    twin = lax.rem(y + 2, 4)
    after, before = lax.rem(section + 1, 4), lax.rem(section + 3, 4)

    small_loads = [
        pltpu.make_async_copy(order_hbm.at[0], order_ref, load_sem.at[5]),
        pltpu.make_async_copy(doc_hbm.at[0], doc_ref, load_sem.at[6]),
        pltpu.make_async_copy(table_hbm, table_ref, load_sem.at[8]),
        pltpu.make_async_copy(gain_hbm, gain_ref, load_sem.at[7]),
    ]
    loads = [
        pltpu.make_async_copy(tok_hbm.at[0, 0], tok, load_sem.at[0]),
        pltpu.make_async_copy(wq_hbm.at[0], wq, load_sem.at[1]),
        pltpu.make_async_copy(wk_hbm.at[0], wk, load_sem.at[2]),
        pltpu.make_async_copy(wv_hbm.at[0], wv, load_sem.at[3]),
    ]
    for load in loads[:1] + small_loads[::-1] + loads[1:]:
        load.start()

    kv_weights = Spread((wk_g, wv_g), x, z, w_ns, w_nr, w_fs, w_fr)
    q_weights = Spread((wq0_g, wq1_g), x, z, wq_ns, wq_nr, wq_fs, wq_fr)
    kvs = Gather((kv0, kv1), x, z, kv_ns, kv_nr, kv_fs, kv_fr)

    barrier = pltpu.get_barrier_semaphore()
    greeted = [kvs.small_device(half, by) for half in range(2)
               for by in (1, -1, 2, -2)]
    greeted += [{"dp": mate}, {"dp": twin}]
    greeted += [{"section": before}, {"section": before, "dp": mate}]
    for device in greeted:
        pl.semaphore_signal(barrier, inc=1, device_id=device, device_id_type=MESH)

    rows0 = pl.ds(pl.multiple_of((lax.rem(z, 4) * 4 + lax.rem(x, 4)) * 64, 64), 64)
    rows1 = pl.ds(pl.multiple_of((lax.rem(x, 4) * 4 + lax.rem(z, 4)) * 64, 64), 64)

    def seed(number, src, dst):
        return pltpu.make_async_remote_copy(
            src_ref=src, dst_ref=dst, send_sem=seed_send.at[number],
            recv_sem=seed_recv.at[number], device_id={"dp": twin}, device_id_type=MESH)

    seeds = [
        seed(0, wk_hbm.at[0, rows0, :], wk_g.at[rows0, :]),
        seed(1, wv_hbm.at[0, rows1, :], wv_g.at[rows1, :]),
        seed(2, wq_hbm.at[0, rows0, pl.ds(0, 256)], wq0_g.at[rows0, :]),
        seed(3, wq_hbm.at[0, rows1, pl.ds(256, 256)], wq1_g.at[rows1, :]),
    ]

    loads[0].wait()
    small_loads[3].wait()
    wide = tok.shape[1] // 4
    square = jnp.zeros((128, 128), F32)
    for column in range(0, tok.shape[1], 128):
        piece = tok[:, column:column + 128].astype(F32)
        square = square + piece * piece
    mean = jnp.sum(square, axis=1, keepdims=True) * (1.0 / tok.shape[1])
    scale = lax.rsqrt(mean + EPSILON)

    def quarter(number):
        columns = pl.ds(pl.multiple_of(number * wide, wide), wide)
        value = tok[:, columns].astype(F32) * scale * gain_ref[:, columns]
        normed[number] = value.astype(BF16)

    def token_copy(slot, number):
        return pltpu.make_async_remote_copy(
            src_ref=normed.at[number], dst_ref=other.at[slot], send_sem=tok_send.at[slot],
            recv_sem=tok_recv.at[slot], device_id={"dp": mate}, device_id_type=MESH)

    token_copies = [token_copy(0, mate), token_copy(1, 3 - y)]
    quarter(mate)

    pl.semaphore_wait(barrier, len(greeted))
    for copy in seeds + token_copies[:1]:
        copy.start()
    quarter(3 - y)
    token_copies[1].start()

    meta_out[...] = jnp.zeros_like(meta_out)
    small_loads[0].wait()
    small_loads[1].wait()
    meta_out[0:1, :] = order_ref[...]
    documents = doc_ref[...]
    for number in range(1, 4):
        count = jnp.sum(jnp.where(documents < number, 1.0, 0.0), axis=1, keepdims=True)
        meta_out[number:number + 1, :] = jnp.broadcast_to(count, (1, 128)).astype(jnp.int32)
    meta_copy = pltpu.make_async_remote_copy(
        src_ref=meta_out, dst_ref=meta_in, send_sem=meta_sem.at[0], recv_sem=meta_sem.at[1],
        device_id={"section": after}, device_id_type=MESH)
    meta_copy.start()

    quarter(y)
    quarter(twin)
    for load in loads[1:]:
        load.wait()

    def own_rows(who, value):
        part[who, :, 0:512] = jnp.dot(value, wq[...], preferred_element_type=F32)
        part[who, :, 512:640] = jnp.dot(value, wk[...], preferred_element_type=F32)
        part[who, :, 640:768] = jnp.dot(value, wv[...], preferred_element_type=F32)

    own_rows(0, normed[y])
    for number in range(4):
        seeds[number].wait_recv()
        (kv_weights, q_weights)[number // 2].begin(number % 2)
    kv_weights.near_steps()
    q_weights.near_steps()
    token_copies[0].wait_recv()
    own_rows(1, other[0])
    kv_weights.arrive(0)
    kv_weights.arrive(1)

    def part_copy(number, who, src, dst):
        device = {"section": after} if who == 0 else {"section": after, "dp": mate}
        return pltpu.make_async_remote_copy(
            src_ref=src.at[who], dst_ref=dst.at[who], send_sem=part_send.at[number],
            recv_sem=part_recv.at[number], device_id=device, device_id_type=MESH)

    part_copies = [part_copy(who, who, kv_out, kv_in) for who in range(2)]
    part_copies += [part_copy(2 + who, who, q_out, q_in) for who in range(2)]
    for who in (0, 1):
        if who == 1:
            token_copies[1].wait_recv()
        value = normed[twin] if who == 0 else other[1]
        for number, weight in enumerate((wk_g, wv_g)):
            rest = jnp.dot(value, weight[...], preferred_element_type=F32)
            columns = slice(number * 128, (number + 1) * 128)
            kv_out[who, :, columns] = (part[who, :, 512 + number * 128:640 + number * 128] + rest).astype(BF16)
        part_copies[who].start()
    q_weights.arrive(0)
    q_weights.arrive(1)
    for who in (1, 0):
        value = normed[twin] if who == 0 else other[1]
        for number, weight in enumerate((wq0_g, wq1_g)):
            rest = jnp.dot(value, weight[...], preferred_element_type=F32)
            columns = slice(number * 256, (number + 1) * 256)
            q_out[who, :, columns] = (part[who, :, columns] + rest).astype(BF16)
        part_copies[2 + who].start()

    meta_copy.wait_recv()
    small_loads[2].wait()
    to_scalars = pltpu.make_async_copy(meta_in, meta_s, load_sem.at[4])
    to_scalars.start()
    to_scalars.wait()

    def block_of(slot_z, slot_x, half):
        return meta_s[0, (slot_z * RING + slot_x) * 2 + half]

    lane = lax.broadcasted_iota(jnp.int32, (BLOCK, HEAD), 1)
    sign = jnp.where(lane < HEAD // 2, -1.0, 1.0)
    fine_cos = table_ref[256:320, :]
    fine_sin = table_ref[320:384, :]
    turns = []
    for half in range(2):
        block = block_of(z, x, half)
        coarse_cos = table_ref[pl.ds(block, 1), :]
        coarse_sin = table_ref[pl.ds(block + 128, 1), :]
        cosine = coarse_cos * fine_cos - coarse_sin * fine_sin
        sine = (coarse_sin * fine_cos + coarse_cos * fine_sin) * sign
        turns.append((cosine, sine))
        position = block * BLOCK + lax.broadcasted_iota(jnp.int32, (BLOCK, 128), 0)
        low = jnp.zeros((BLOCK, 128), jnp.int32)
        for number in range(1, 4):
            start = meta_in[number:number + 1, :]
            low = jnp.maximum(low, jnp.where(start <= position, start, 0))
        qpos[half * BLOCK:(half + 1) * BLOCK, :] = position
        qlo[half * BLOCK:(half + 1) * BLOCK, :] = low

    def turned(value, half):
        cosine, sine = turns[half]
        return value * cosine + pltpu.roll(value, HEAD // 2, 1) * sine

    for copy in part_copies[:2]:
        copy.wait_recv()
    for half in range(2):
        rows = slice(half * BLOCK, (half + 1) * BLOCK)
        both = kv_in[0, rows, :].astype(F32) + kv_in[1, rows, :].astype(F32)
        big = z if half == 0 else x
        slot = pl.ds(pl.multiple_of(big * RING * BLOCK, BLOCK), BLOCK)
        buffer = kv0 if half == 0 else kv1
        buffer[slot, 0:128] = turned(both[:, 0:128], half).astype(BF16)
        buffer[slot, 128:256] = both[:, 128:256].astype(BF16)
        kvs.begin(half)
    kv_weights.finish()
    q_weights.finish()
    for copy in seeds + token_copies + [meta_copy]:
        copy.wait_send()

    run_max[...] = jnp.full(run_max.shape, FLOOR, F32)
    acc[...] = jnp.zeros_like(acc)
    kvs.near_step(1)
    kvs.near_step(2)
    kvs.arrive(1, 0)
    kvs.near_step(3)
    kvs.arrive(1, 1)
    kvs.arrive(2, 0)
    kvs.near_step(4)
    for copy in part_copies[2:]:
        copy.wait_recv()
    for copy in part_copies:
        copy.wait_send()
    for half in range(2):
        rows = slice(half * BLOCK, (half + 1) * BLOCK)
        for head in range(4):
            columns = slice(head * HEAD, (head + 1) * HEAD)
            both = q_in[0, rows, columns].astype(F32) + q_in[1, rows, columns].astype(F32)
            q_ref[head, rows, :] = turned(both, half).astype(BF16)

    scaling = math.log2(math.e) * HEAD ** -0.5
    lanes = lax.broadcasted_iota(jnp.int32, (1, 128), 1)
    inner = lax.rem(lanes, BLOCK)
    first = lanes < BLOCK

    def tile(t, carry):
        one_row = (t == 0) | (t == 7)
        hop = jnp.where(t == 0, 0, jnp.where((t == 1) | (t == 3), 1, jnp.where(
            (t == 2) | (t == 5), 2, jnp.where(t == 7, 4, 3))))
        half_row = jnp.where((t == 3) | (t == 5) | (t == 6), 1, 0)
        due = {1: [(1, 2)], 2: [(2, 1), (3, 0), (1, 3)], 3: [(2, 2)], 4: [(3, 1), (2, 3)],
               5: [(3, 2)], 6: [(3, 3)], 7: [(4, 0), (4, 1), (4, 2), (4, 3)]}
        for number, pieces in due.items():
            @pl.when(t == number)
            def _(pieces=pieces, number=number):
                if number == 6:
                    kvs.drain((1, 2), near=True)
                if number == 7:
                    kvs.drain((3,))
                for piece in pieces:
                    kvs.arrive(*piece)

        keys, values = [], []
        for half in range(2):
            for way in range(2):
                big = wrap(kvs.big[half] - hop * (1 - 2 * way))
                small = 4 * jnp.where(one_row, way, half_row)
                begin = pl.multiple_of((big * RING + small) * BLOCK, 4 * BLOCK)
                buffer = kv0 if half == 0 else kv1
                both = buffer[pl.ds(begin, 4 * BLOCK), :]
                keys.append(both[:, 0:128])
                values.append(both[:, 128:256])
                for pair in range(2):
                    numbers = []
                    for k in range(2):
                        index = small + 2 * pair + k
                        offset = (index + 1) // 2 * (1 - 2 * lax.rem(index, 2))
                        inside = wrap(kvs.small[half] + offset)
                        if half == 0:
                            numbers.append(block_of(big, inside, 0))
                        else:
                            numbers.append(block_of(inside, big, 1))
                    position = jnp.where(first, numbers[0], numbers[1]) * BLOCK + inner
                    column = (half * 2 + way) * 256 + pair * 128
                    allowed = (position <= qpos[...]) & (position >= qlo[...])
                    bias[:, column:column + 128] = jnp.where(allowed, 0.0, MASKED)
        key = jnp.concatenate(keys, axis=0)
        value = jnp.concatenate(values, axis=0)
        value = jnp.concatenate([value, jnp.ones_like(value)], axis=1)
        for head in range(4):
            scores = lax.dot_general(q_ref[head], key, (((1,), (1,)), ((), ())),
                                     preferred_element_type=F32)
            scores = scores * scaling + bias[...]
            old = run_max[head]
            new = jnp.maximum(old, jnp.max(scores, axis=1, keepdims=True))
            run_max[head] = new
            probs = jnp.exp2(scores - new[:, 0:1]).astype(BF16)
            factor = jnp.exp2(old - new)
            got = jnp.dot(probs, value, preferred_element_type=F32)
            acc[head, :, 0:128] = acc[head, :, 0:128] * factor + got[:, 0:128]
            acc[head, :, 128:256] = acc[head, :, 128:256] * factor + got[:, 128:256]
        return carry

    lax.fori_loop(0, 8, tile, 0)

    for head in range(4):
        result = acc[head, :, 0:128] / acc[head, :, 128:256]
        out_ref[:, head * HEAD:(head + 1) * HEAD] = result.astype(BF16)

    kvs.drain((4,))


def local(tokens, norm_gain, query_weight, key_weight, value_weight, block_order, doc_ids):
    width = tokens.shape[3]
    deep = width // 4
    table = jnp.asarray(rope_tables())
    hbm = pl.BlockSpec(memory_space=pltpu.HBM)
    vmem = pl.BlockSpec(memory_space=pltpu.VMEM)
    dma = pltpu.SemaphoreType.DMA
    out = pl.pallas_call(
        kernel,
        out_shape=jax.ShapeDtypeStruct((128, 512), BF16),
        in_specs=[hbm] * 8,
        out_specs=vmem,
        scratch_shapes=[
            pltpu.VMEM((1, width), F32),
            pltpu.VMEM((1, 128), jnp.int32),
            pltpu.VMEM((1, doc_ids.shape[2]), jnp.int32),
            pltpu.VMEM(table.shape, F32),
            pltpu.VMEM((128, width), BF16),
            pltpu.VMEM((4, 128, deep), BF16),
            pltpu.VMEM((2, 128, deep), BF16),
            pltpu.VMEM((deep, 512), BF16),
            pltpu.VMEM((deep, 128), BF16),
            pltpu.VMEM((deep, 128), BF16),
            pltpu.VMEM((deep, 128), BF16),
            pltpu.VMEM((deep, 128), BF16),
            pltpu.VMEM((deep, 256), BF16),
            pltpu.VMEM((deep, 256), BF16),
            pltpu.VMEM((2, 128, 768), F32),
            pltpu.VMEM((2, 128, 256), BF16),
            pltpu.VMEM((2, 128, 512), BF16),
            pltpu.VMEM((2, 128, 256), BF16),
            pltpu.VMEM((2, 128, 512), BF16),
            pltpu.VMEM((64 * BLOCK, 256), BF16),
            pltpu.VMEM((64 * BLOCK, 256), BF16),
            pltpu.VMEM((8, 128), jnp.int32),
            pltpu.VMEM((8, 128), jnp.int32),
            pltpu.SMEM((8, 128), jnp.int32),
            pltpu.VMEM((4, 128, 128), BF16),
            pltpu.VMEM((128, 128), jnp.int32),
            pltpu.VMEM((128, 128), jnp.int32),
            pltpu.VMEM((4, 128, 128), F32),
            pltpu.VMEM((4, 128, 256), F32),
            pltpu.VMEM((128, 1024), F32),
            dma((9,)), dma((2,)), dma((4,)), dma((4,)), dma((2,)), dma((2,)), dma((4,)), dma((4,)),
            dma((2, 4)), dma((2, 4)), dma((2, 3, 4)), dma((2, 3, 4)),
            dma((2, 4)), dma((2, 4)), dma((2, 3, 4)), dma((2, 3, 4)),
            dma((2, 2, 4)), dma((2, 2, 4)), dma((2, 2, 4, 4)), dma((2, 2, 4, 4)),
        ],
        compiler_params=pltpu.CompilerParams(
            collective_id=0, has_side_effects=True, vmem_limit_bytes=63 * 1024 * 1024),
        name="relay_attention",
    )(tokens, norm_gain, query_weight, key_weight, value_weight, block_order, doc_ids, table)
    return out[None, None]


def solution(mesh):
    in_specs = (
        P("section", "dp", "ctx", None),
        P("section", None),
        P("section", "dp", None),
        P("section", "dp", None),
        P("section", "dp", None),
        P("section", "dp", None),
        P("section", "dp", None),
    )
    out_specs = P("section", "dp", "ctx", None)
    return jax.shard_map(local, mesh=mesh, in_specs=in_specs, out_specs=out_specs, check_vma=False)
```
